512 devices in a mesh: dp: 4 (over z_lo), blk: 16 (over z_hi, y), uly: 8 (over x, core).
Axes of the slice: x: 4, y: 8, z: 8 (z_hi: 2, z_lo: 4; z = z_hi * 4 + z_lo), core: 2. Of those that a mesh axis runs over, the one named last changes fastest.
Arguments:
- queries: bfloat16 [4, 16384, 1024], P('dp', ('blk', 'uly')), may hold values from -6 to 6
- key_vectors: bfloat16 [4, 16384, 1024], P('dp', ('blk', 'uly')), may hold values from -6 to 6
- value_vectors: bfloat16 [4, 16384, 1024], P('dp', ('blk', 'uly')), may hold values from -6 to 6
- grad_context: bfloat16 [4, 16384, 1024], P('dp', ('blk', 'uly')), may hold values from -6 to 6
- content_bias: float32 [16, 64], P('uly'), may hold values from -3 to 3
- slopes: float32 [16], P('uly'), may hold values from 0.002 to 0.1
- lengths: int32 [4], P('dp'), may hold values from 4096 to 16384, as said below
Outputs:
- context: bfloat16 [4, 16384, 1024], P('dp', ('blk', 'uly'))
- grad_queries: bfloat16 [4, 16384, 1024], P('dp', ('blk', 'uly'))
- grad_keys: bfloat16 [4, 16384, 1024], P('dp', ('blk', 'uly'))
- grad_values: bfloat16 [4, 16384, 1024], P('dp', ('blk', 'uly'))
- grad_bias: float32 [16, 64], P('uly')
- grad_slopes: float32 [16], P('uly')
The draws below stay inside these ranges and needn't reach their ends.
Inputs may be any that keep to these rules, and one draw needn't show every extreme that they name: `lengths`: frames at or beyond a recording's length are padding; at least one recording of the batch has all 16384 frames valid.
All inputs are finite; a program needn't handle non-finite values.
Results may differ from the reference program's by a relative error of at most 0.012.
The reference program's roundings to bfloat16 on the way (of `query_bias`, `upstream`, `soft_weights` and `scaled_grads`) count: a program that leaves them out, or rounds other values in their place, can miss the bound.
Values may be sent and summed in bfloat16 or wider, within the bound.
No kernel may reach another device: no remote copies, remote signals or barrier semaphores. Data moves between devices by JAX's collectives and lax.ppermute only.
A program may use at most 64 MiB of HBM per device.

```python
import math
import jax
import jax.numpy as jnp
from jax import lax

HEADS = 16
HEAD_DIM = 64
LEN = 16384
BATCH = 4
CTX = 1024
HD = 1024


def draw_queries(key, part):
    key = jax.random.fold_in(key, 1)
    drawn_draw = jax.random.truncated_normal(key, -6.0, 6.0, (BATCH, LEN, HD), jnp.float32)
    return drawn_draw.astype(jnp.bfloat16)


def draw_key_vectors(key, part):
    key = jax.random.fold_in(key, 2)
    drawn_draw = jax.random.truncated_normal(key, -6.0, 6.0, (BATCH, LEN, HD), jnp.float32)
    return drawn_draw.astype(jnp.bfloat16)


def draw_lengths(key, part):
    key = jax.random.fold_in(key, 3)
    drawn = jax.random.randint(key, (BATCH,), LEN // 4, LEN + 1)
    full_row = jax.random.randint(jax.random.fold_in(key, 4), (), 0, BATCH)
    return jnp.where(jnp.arange(BATCH) == full_row, LEN, drawn).astype(jnp.int32)


def block_scale(stream_key, extent, pieces, smallest, high):
    loudness, own = 1.0, jax.random.fold_in(stream_key, 6)
    for dim, blocks in pieces:
        draws = jnp.exp(jax.random.uniform(jax.random.fold_in(own, dim), (blocks,), jnp.float32, smallest / len(pieces), high / len(pieces)))
        loudness = loudness * jnp.repeat(draws, extent[dim] // blocks).reshape([-1 if axis == dim else 1 for axis in range(len(extent))])
    return loudness


def gaussian(own_key, extent, deviation, bound, split=(), kind=jnp.bfloat16):
    values = jax.random.normal(own_key, extent, jnp.float32) * deviation
    if len(split) > 0:
        values = block_scale(own_key, extent, split, -0.22, 0.18) * values
    return jnp.clip(values, min=-bound, max=bound).astype(kind)


def setup_inputs(seed: int = 0) -> dict:
    arg_keys = jax.random.split(jax.random.key(seed), 8)
    queries = draw_queries(jax.random.fold_in(arg_keys[7], 71), 0)
    key_vectors = draw_key_vectors(jax.random.fold_in(arg_keys[7], 71), 0)
    value_vectors = gaussian(arg_keys[2], (BATCH, LEN, HD), 1.0, 6.0, ((0, 4), (1, 128)))
    grad_context = gaussian(arg_keys[3], (BATCH, LEN, HD), 1.0, 6.0, ((0, 4), (1, 128)))
    content_bias = gaussian(arg_keys[4], (HEADS, HEAD_DIM), 0.5, 3.0, ((0, 8),), jnp.float32)
    slopes = jnp.clip(jnp.exp(math.log(0.1) - 3.912023 * jax.random.uniform(arg_keys[5], (HEADS,), jnp.float32) ** block_scale(arg_keys[5], (HEADS,), ((0, 8),), -0.2, 0.2)), 0.002, 0.1)
    lengths = draw_lengths(jax.random.fold_in(arg_keys[7], 71), 0)
    return dict(queries=queries, key_vectors=key_vectors, value_vectors=value_vectors, grad_context=grad_context, content_bias=content_bias, slopes=slopes, lengths=lengths)


masked_score = -1e30


def head_terms(query_rows, key_rows, value_rows, upstream_rows, bias_row, slope_value, length):
    factor = HEAD_DIM ** -0.5
    tile_rows = min(512, LEN)
    window = tile_rows + 2 * CTX
    frames = jnp.arange(LEN, dtype=jnp.int32)
    query_bias = (query_rows.astype(jnp.float32) + bias_row[None, :]).astype(jnp.bfloat16)
    upstream = jnp.where((frames < length)[:, None], upstream_rows, jnp.zeros_like(upstream_rows))
    zero_rows = jnp.zeros((CTX, HEAD_DIM), jnp.bfloat16)
    key_pad = jnp.concatenate([zero_rows, key_rows, zero_rows], axis=0)
    value_pad = jnp.concatenate([zero_rows, value_rows, zero_rows], axis=0)

    def tile_step(running, offset):
        key_acc, value_acc = running
        query_tile = lax.dynamic_slice_in_dim(query_bias, offset, tile_rows, 0)
        upstream_tile = lax.dynamic_slice_in_dim(upstream, offset, tile_rows, 0)
        key_win = lax.dynamic_slice_in_dim(key_pad, offset, window, 0)
        value_win = lax.dynamic_slice_in_dim(value_pad, offset, window, 0)
        query_place = offset + jnp.arange(tile_rows, dtype=jnp.int32)
        key_place = offset - CTX + jnp.arange(window, dtype=jnp.int32)
        spacing = jnp.abs(query_place[:, None] - key_place[None, :])
        usable = (spacing <= CTX) & (key_place[None, :] >= 0) & (key_place[None, :] < length)
        distance = spacing.astype(jnp.float32)
        scores = jnp.dot(query_tile, key_win.T, preferred_element_type=jnp.float32) * factor
        scores = jnp.where(usable, scores - slope_value * distance, masked_score)
        row_max = jnp.max(scores, axis=1, keepdims=True)
        powers = jnp.exp(scores - row_max)
        attention = powers / jnp.sum(powers, axis=1, keepdims=True)
        soft_weights = attention.astype(jnp.bfloat16)
        context = jnp.dot(soft_weights, value_win, preferred_element_type=jnp.float32)
        context = jnp.where((query_place < length)[:, None], context, jnp.zeros_like(context))
        dot_grads = jnp.dot(upstream_tile, value_win.T, preferred_element_type=jnp.float32)
        row_delta = jnp.sum(attention * dot_grads, axis=1, keepdims=True)
        score_grads = attention * (dot_grads - row_delta)
        scaled_grads = (score_grads * factor).astype(jnp.bfloat16)
        query_grad = jnp.dot(scaled_grads, key_win, preferred_element_type=jnp.float32)
        slope_grad = -jnp.sum(score_grads * distance)
        key_part = jnp.dot(scaled_grads.T, query_tile, preferred_element_type=jnp.float32)
        value_part = jnp.dot(soft_weights.T, upstream_tile, preferred_element_type=jnp.float32)
        key_acc = lax.dynamic_update_slice_in_dim(key_acc, lax.dynamic_slice_in_dim(key_acc, offset, window, 0) + key_part, offset, 0)
        value_acc = lax.dynamic_update_slice_in_dim(value_acc, lax.dynamic_slice_in_dim(value_acc, offset, window, 0) + value_part, offset, 0)
        return (key_acc, value_acc), (context.astype(jnp.bfloat16), query_grad, slope_grad)

    zero_grads = jnp.zeros((LEN + 2 * CTX, HEAD_DIM), jnp.float32)
    offsets = jnp.arange(LEN // tile_rows, dtype=jnp.int32) * tile_rows
    (key_acc, value_acc), (contexts, query_grads, slope_grads) = lax.scan(tile_step, (zero_grads, zero_grads), offsets)
    query_grads = query_grads.reshape(LEN, HEAD_DIM)
    return (contexts.reshape(LEN, HEAD_DIM), query_grads.astype(jnp.bfloat16),
            key_acc[CTX:CTX + LEN].astype(jnp.bfloat16), value_acc[CTX:CTX + LEN].astype(jnp.bfloat16),
            jnp.sum(query_grads, axis=0), jnp.sum(slope_grads))


def split_heads(array):
    return array.reshape(LEN, HEADS, HEAD_DIM).transpose(1, 0, 2)


def join_heads(array):
    return array.transpose(1, 0, 2).reshape(LEN, HD)


def reference(queries, key_vectors, value_vectors, grad_context, content_bias, slopes, lengths):
    contexts, query_out, key_out, value_out = [], [], [], []
    bias_total = jnp.zeros((HEADS, HEAD_DIM), jnp.float32)
    slope_total = jnp.zeros((HEADS,), jnp.float32)
    for batch_row in range(BATCH):
        length = lengths[batch_row]

        def per_head(packed):
            query_rows, key_rows, value_rows, upstream_rows, bias_row, slope_value = packed
            return head_terms(query_rows, key_rows, value_rows, upstream_rows, bias_row, slope_value, length)

        results = lax.map(per_head, (split_heads(queries[batch_row]), split_heads(key_vectors[batch_row]),
                                     split_heads(value_vectors[batch_row]), split_heads(grad_context[batch_row]),
                                     content_bias, slopes))
        contexts.append(join_heads(results[0]))
        query_out.append(join_heads(results[1]))
        key_out.append(join_heads(results[2]))
        value_out.append(join_heads(results[3]))
        bias_total = bias_total + results[4]
        slope_total = slope_total + results[5]
    return (jnp.stack(contexts), jnp.stack(query_out), jnp.stack(key_out), jnp.stack(value_out), bias_total, slope_total)
```

```python
import jax
import jax.numpy as jnp
from jax import lax
from jax.experimental import pallas as pl
from jax.experimental.pallas import tpu as pltpu
from jax.sharding import PartitionSpec as P

BLOCK = 1024
TILE = 256
HALO = BLOCK + TILE
PEERS = 8
CHUNK = BLOCK // PEERS
LANES = 128
HEAD = 64
FACTOR = HEAD**-0.5
LOG2E = 1.4426950408889634
FAR = 1e30
VMEM_LIMIT = 56 * 1024 * 1024
F32 = jnp.float32
BF16 = jnp.bfloat16


def iota(shape, dim):
    return lax.broadcasted_iota(jnp.int32, shape, dim)


def dot_nt(a, b):
    return lax.dot_general(a, b, (((1,), (1,)), ((), ())), preferred_element_type=F32)


def dot_nn(a, b):
    return jnp.dot(a, b, preferred_element_type=F32)


def own_lanes(head, shape):
    lane = iota(shape, 1)
    return lane < HEAD if head == 0 else lane >= HEAD


def spare(head):
    return HEAD if head == 0 else 0


def fill_keys(kv_ref, keys, values, base, start, length):
    shape = (CHUNK, LANES)
    lane = iota(shape, 1)
    for peer in range(PEERS):
        rows = pl.ds(base + peer * CHUNK, CHUNK)
        place = start + peer * CHUNK + iota(shape, 0)
        blocked = jnp.where((place >= 0) & (place < length), 0.0, -FAR)
        key = kv_ref[peer, 0].astype(F32)
        value = kv_ref[peer, 1].astype(F32)
        for head in range(2):
            own, at = own_lanes(head, shape), spare(head)
            keys[head, rows] = jnp.where(own, key, jnp.where(lane == at, blocked, 0.0)).astype(BF16)
            ones = ((lane >= at) & (lane < at + 3)).astype(F32)
            values[head, rows] = jnp.where(own, value, ones).astype(BF16)


def fill_penalty(slopes_ref, penalty):
    for head in range(2):
        slope = slopes_ref[head] * LOG2E
        for piece in range((2 * BLOCK + TILE) // TILE):
            spacing = jnp.abs(iota((TILE, TILE), 0) + BLOCK - piece * TILE - iota((TILE, TILE), 1))
            penalty[head, :, pl.ds(piece * TILE, TILE)] = jnp.where(
                spacing <= BLOCK, spacing.astype(F32) * slope, FAR
            )


def load_queries(qd_ref, bias_ref):
    query = jnp.concatenate([qd_ref[0, 0], qd_ref[1, 0]], axis=0).astype(F32)
    return (query + bias_ref[...]).astype(BF16).astype(F32)


def load_upstream(qd_ref, first, length):
    upstream = jnp.concatenate([qd_ref[0, 1], qd_ref[1, 1]], axis=0).astype(F32)
    place = first + iota((TILE, LANES), 0)
    return jnp.where(place < length, upstream, 0.0)


def with_spare(head, rows, columns):
    lane = iota((TILE, LANES), 1)
    other = jnp.zeros((TILE, LANES), F32)
    for k, column in enumerate(columns):
        other = jnp.where(lane == spare(head) + k, column, other)
    return jnp.where(own_lanes(head, (TILE, LANES)), rows, other)


def thirds(column):
    high = column.astype(BF16).astype(F32)
    middle = (column - high).astype(BF16).astype(F32)
    return high, middle, column - high - middle


def centre_forward(meta, slopes_ref, kv_ref, qd_ref, bias_ref, p_ref, o_ref, keys, values, penalty):
    tile = pl.program_id(0)

    @pl.when(tile == 0)
    def _():
        fill_keys(kv_ref, keys, values, 0, meta[0], meta[1])
        fill_penalty(slopes_ref, penalty)

    query = load_queries(qd_ref, bias_ref)
    for head in range(2):
        at = spare(head)
        rows = with_spare(head, query, (1.0,)).astype(BF16)
        shift = pl.multiple_of(BLOCK - tile * TILE, TILE)
        scores = dot_nt(rows, keys[head]) * (FACTOR * LOG2E) - penalty[head, :, pl.ds(shift, BLOCK)]
        top = jnp.max(scores, axis=1, keepdims=True)
        powers = jnp.exp2(scores - top).astype(BF16)
        p_ref[head] = powers
        out = dot_nn(powers, values[head])
        o_ref[head] = jnp.where(iota((TILE, LANES), 1) == at + 1, top, out)


def halo_both(
    meta,
    slopes_ref,
    low_ref,
    high_ref,
    qd_ref,
    bias_ref,
    o_ref,
    ctx_ref,
    dq_ref,
    stat_ref,
    dlow_ref,
    dhigh_ref,
    slope_ref,
    keys,
    values,
    penalty,
    dkt,
    dvt,
):
    tile = pl.program_id(0)
    first, length = meta[0], meta[1]

    @pl.when(tile == 0)
    def _():
        fill_keys(low_ref, keys, values, 0, first - BLOCK, length)
        fill_keys(high_ref, keys, values, BLOCK, first + BLOCK, length)
        fill_penalty(slopes_ref, penalty)
        dkt[...] = jnp.zeros_like(dkt)
        dvt[...] = jnp.zeros_like(dvt)
        slope_ref[...] = jnp.zeros_like(slope_ref)

    query = load_queries(qd_ref, bias_ref)
    upstream = load_upstream(qd_ref, first + tile * TILE, length)
    begin = pl.multiple_of(tile * TILE, TILE)
    span = pl.ds(begin, HALO)
    shape = (TILE, LANES)
    lane = iota(shape, 1)
    context = jnp.zeros(shape, F32)
    dq = jnp.zeros(shape, F32)
    stats = jnp.zeros(shape, F32)
    inverses, weights, grads = [], [], []
    for head in range(2):
        at, own = spare(head), own_lanes(head, shape)
        rows = with_spare(head, query, (1.0,)).astype(BF16)
        key_win = keys[head, span]
        value_win = values[head, span]
        pieces = []
        for piece in range(HALO // TILE):
            shift = jnp.where(piece < BLOCK // TILE - tile, piece * TILE, piece * TILE + BLOCK)
            pieces.append(penalty[head, :, pl.ds(pl.multiple_of(shift, TILE), TILE)])
        far = jnp.concatenate(pieces, axis=1)
        scores = dot_nt(rows, key_win) * (FACTOR * LOG2E) - far
        held = o_ref[head]
        top_held = held[:, at + 1 : at + 2]
        top = jnp.maximum(top_held, jnp.max(scores, axis=1, keepdims=True))
        powers = jnp.exp2(scores - top).astype(BF16)
        kept = jnp.exp2(top_held - top)
        out = held * kept + dot_nn(powers, value_win)
        inverse = 1.0 / out[:, at : at + 1]
        out = out * inverse
        delta = jnp.sum(jnp.where(own, upstream * out, 0.0), axis=1, keepdims=True)
        context = jnp.where(own, out, context)
        up_rows = with_spare(head, upstream, thirds(-delta)).astype(BF16)
        slope_grads = powers.astype(F32) * dot_nt(up_rows, value_win)
        score_grads = slope_grads.astype(BF16)
        dq = jnp.where(own, dot_nn(score_grads, key_win) * (inverse * FACTOR), dq)
        by_lane = jnp.zeros(shape, F32)
        weighted = slope_grads * far
        for piece in range(HALO // LANES):
            by_lane = by_lane + weighted[:, piece * LANES : (piece + 1) * LANES]
        slope_ref[pl.ds(head * 8, 8)] += jnp.broadcast_to(
            jnp.sum(by_lane * inverse, axis=0, keepdims=True), (8, LANES)
        )
        stats = jnp.where(lane == 2 * head, delta, stats)
        stats = jnp.where(lane == 2 * head + 1, kept * inverse, stats)
        inverses.append(inverse)
        weights.append(powers)
        grads.append(score_grads)
    place = first + tile * TILE + iota(shape, 0)
    ctx_ref[...] = jnp.where(place < length, context, 0.0).astype(BF16)
    dq_ref[...] = dq
    stat_ref[...] = stats
    inverse = jnp.where(lane < HEAD, inverses[0], inverses[1])
    up_cols = (upstream * inverse).T.astype(BF16)
    query_cols = (query * (inverse * FACTOR)).T.astype(BF16)
    for head in range(2):
        part = pl.ds(head * HEAD, HEAD)
        half = slice(head * HEAD, (head + 1) * HEAD)
        dvt[part, span] += dot_nn(up_cols[half], weights[head])
        dkt[part, span] += dot_nn(query_cols[half], grads[head])

    @pl.when(tile == BLOCK // TILE - 1)
    def _():
        for peer in range(PEERS):
            for side, out_ref in ((0, dlow_ref), (BLOCK, dhigh_ref)):
                cols = pl.ds(side + peer * CHUNK, CHUNK)
                out_ref[peer, 0] = dkt[:, cols].T.astype(BF16)
                out_ref[peer, 1] = dvt[:, cols].T.astype(BF16)


def centre_backward(
    meta,
    slopes_ref,
    kv_ref,
    qd_ref,
    bias_ref,
    p_ref,
    stat_ref,
    ctx_ref,
    dq_ref,
    halo_slope_ref,
    cq_ref,
    dkv_ref,
    sums_ref,
    keys,
    values,
    penalty,
    dkt,
    dvt,
    slope_acc,
):
    tile = pl.program_id(0)
    first, length = meta[0], meta[1]

    @pl.when(tile == 0)
    def _():
        fill_keys(kv_ref, keys, values, 0, first, length)
        fill_penalty(slopes_ref, penalty)
        dkt[...] = jnp.zeros_like(dkt)
        dvt[...] = jnp.zeros_like(dvt)
        slope_acc[...] = halo_slope_ref[...]
        sums_ref[...] = jnp.zeros_like(sums_ref)

    query = load_queries(qd_ref, bias_ref)
    upstream = load_upstream(qd_ref, first + tile * TILE, length)
    shift = pl.multiple_of(BLOCK - tile * TILE, TILE)
    shape = (TILE, LANES)
    lane = iota(shape, 1)
    dq = dq_ref[...]
    stats = stat_ref[...]
    scales = [stats[:, 2 * head + 1 : 2 * head + 2] for head in range(2)]
    scale = jnp.where(lane < HEAD, scales[0], scales[1])
    up_cols = (upstream * scale).T.astype(BF16)
    query_cols = (query * (scale * FACTOR)).T.astype(BF16)
    for head in range(2):
        own = own_lanes(head, shape)
        delta = stats[:, 2 * head : 2 * head + 1]
        up_rows = with_spare(head, upstream, thirds(-delta)).astype(BF16)
        powers = p_ref[head]
        slope_grads = powers.astype(F32) * dot_nt(up_rows, values[head])
        score_grads = slope_grads.astype(BF16)
        dq = dq + jnp.where(own, dot_nn(score_grads, keys[head]) * (scales[head] * FACTOR), 0.0)
        weighted = slope_grads * penalty[head, :, pl.ds(shift, BLOCK)]
        by_lane = jnp.zeros(shape, F32)
        for piece in range(BLOCK // LANES):
            by_lane = by_lane + weighted[:, piece * LANES : (piece + 1) * LANES]
        slope_acc[pl.ds(head * 8, 8)] += jnp.broadcast_to(
            jnp.sum(by_lane * scales[head], axis=0, keepdims=True), (8, LANES)
        )
        part = pl.ds(head * HEAD, HEAD)
        half = slice(head * HEAD, (head + 1) * HEAD)
        dvt[part] += dot_nn(up_cols[half], powers)
        dkt[part] += dot_nn(query_cols[half], score_grads)
    for half in range(2):
        rows = slice(half * CHUNK, (half + 1) * CHUNK)
        cq_ref[half, 0] = ctx_ref[rows]
        cq_ref[half, 1] = dq[rows].astype(BF16)
    sums_ref[0:1] += jnp.sum(dq, axis=0, keepdims=True)

    @pl.when(tile == BLOCK // TILE - 1)
    def _():
        row = iota((1, LANES), 1)
        totals = []
        for head in range(2):
            total = jnp.sum(slope_acc[pl.ds(head * 8, 1)], axis=1, keepdims=True)
            totals.append(-total / (slopes_ref[head] * LOG2E))
        sums_ref[1:2] = jnp.where(row == 0, totals[0], jnp.where(row == 1, totals[1], 0.0))
        for peer in range(PEERS):
            cols = pl.ds(peer * CHUNK, CHUNK)
            dkv_ref[peer, 0] = dkt[:, cols].T
            dkv_ref[peer, 1] = dvt[:, cols].T


SMEM = pl.BlockSpec(memory_space=pltpu.SMEM)
TILES = BLOCK // TILE


def whole(*shape):
    return pl.BlockSpec(shape, lambda tile: (0,) * len(shape))


def spec_rows(*shape):
    return pl.BlockSpec(shape, lambda tile: (tile,) + (0,) * (len(shape) - 1))


def spec_heads(width):
    return pl.BlockSpec((2, TILE, width), lambda tile: (0, tile, 0))


PAIR = (PEERS, 2, CHUNK, LANES)
PAIR_TILE = (2, 2, CHUNK, LANES)


def params():
    return pltpu.CompilerParams(
        dimension_semantics=("arbitrary",), vmem_limit_bytes=VMEM_LIMIT
    )


def cost(keys, products):
    pairs = 2 * BLOCK * keys
    return pl.CostEstimate(
        flops=2 * pairs * LANES * products, bytes_accessed=8 * 1024 * 1024, transcendentals=pairs
    )


def shaped(shape, kind):
    return jax.ShapeDtypeStruct(shape, kind)


def run_centre_forward(meta, slopes, kv, qd, bias):
    return pl.pallas_call(
        centre_forward,
        grid=(TILES,),
        in_specs=[SMEM, SMEM, whole(*PAIR), spec_rows(*PAIR_TILE), whole(1, LANES)],
        out_specs=[spec_heads(BLOCK), spec_heads(LANES)],
        out_shape=[shaped((2, BLOCK, BLOCK), BF16), shaped((2, BLOCK, LANES), F32)],
        scratch_shapes=[
            pltpu.VMEM((2, BLOCK, LANES), BF16),
            pltpu.VMEM((2, BLOCK, LANES), BF16),
            pltpu.VMEM((2, TILE, 2 * BLOCK + TILE), F32),
        ],
        compiler_params=params(),
        cost_estimate=cost(BLOCK, 2),
        name="centre_forward",
    )(meta, slopes, kv, qd, bias)


def run_halo(meta, slopes, low, high, qd, bias, held):
    return pl.pallas_call(
        halo_both,
        grid=(TILES,),
        in_specs=[
            SMEM,
            SMEM,
            whole(*PAIR),
            whole(*PAIR),
            spec_rows(*PAIR_TILE),
            whole(1, LANES),
            spec_heads(LANES),
        ],
        out_specs=[
            spec_rows(TILE, LANES),
            spec_rows(TILE, LANES),
            spec_rows(TILE, LANES),
            whole(*PAIR),
            whole(*PAIR),
            whole(16, LANES),
        ],
        out_shape=[
            shaped((BLOCK, LANES), BF16),
            shaped((BLOCK, LANES), F32),
            shaped((BLOCK, LANES), F32),
            shaped(PAIR, BF16),
            shaped(PAIR, BF16),
            shaped((16, LANES), F32),
        ],
        scratch_shapes=[
            pltpu.VMEM((2, 2 * BLOCK, LANES), BF16),
            pltpu.VMEM((2, 2 * BLOCK, LANES), BF16),
            pltpu.VMEM((2, TILE, 2 * BLOCK + TILE), F32),
            pltpu.VMEM((LANES, 2 * BLOCK), F32),
            pltpu.VMEM((LANES, 2 * BLOCK), F32),
        ],
        compiler_params=params(),
        cost_estimate=cost(HALO, 6),
        name="halo_both",
    )(meta, slopes, low, high, qd, bias, held)


def run_centre_backward(meta, slopes, kv, qd, bias, powers, stats, context, dq, halo_slope):
    return pl.pallas_call(
        centre_backward,
        grid=(TILES,),
        in_specs=[
            SMEM,
            SMEM,
            whole(*PAIR),
            spec_rows(*PAIR_TILE),
            whole(1, LANES),
            spec_heads(BLOCK),
            spec_rows(TILE, LANES),
            spec_rows(TILE, LANES),
            spec_rows(TILE, LANES),
            whole(16, LANES),
        ],
        out_specs=[spec_rows(*PAIR_TILE), whole(*PAIR), whole(2, LANES)],
        out_shape=[shaped(PAIR, BF16), shaped(PAIR, F32), shaped((2, LANES), F32)],
        scratch_shapes=[
            pltpu.VMEM((2, BLOCK, LANES), BF16),
            pltpu.VMEM((2, BLOCK, LANES), BF16),
            pltpu.VMEM((2, TILE, 2 * BLOCK + TILE), F32),
            pltpu.VMEM((LANES, BLOCK), F32),
            pltpu.VMEM((LANES, BLOCK), F32),
            pltpu.VMEM((16, LANES), F32),
        ],
        compiler_params=params(),
        cost_estimate=cost(BLOCK, 4),
        name="centre_backward",
    )(meta, slopes, kv, qd, bias, powers, stats, context, dq, halo_slope)


def split_pair(first_ref, second_ref, out_ref):
    for peer in range(PEERS):
        cols = pl.ds(peer * LANES, LANES)
        out_ref[peer, 0] = first_ref[0, :, cols]
        out_ref[peer, 1] = second_ref[0, :, cols]


def run_split(first, second):
    return pl.pallas_call(split_pair, out_shape=shaped(PAIR, BF16), name="split_pair")(first, second)


def join_pair(pair_ref, first_ref, second_ref):
    for peer in range(PEERS):
        cols = pl.ds(peer * LANES, LANES)
        first_ref[0, :, cols] = pair_ref[peer, 0]
        second_ref[0, :, cols] = pair_ref[peer, 1]


def run_join(pair):
    whole_rows = shaped((1, CHUNK, PEERS * LANES), BF16)
    return pl.pallas_call(join_pair, out_shape=[whole_rows, whole_rows], name="join_pair")(pair)


def across(pair):
    return lax.all_to_all(pair, "uly", split_axis=0, concat_axis=0, tiled=True)


def from_behind(block, distance):
    count = lax.axis_size("blk")
    route = [(i - distance, i) for i in range(count) if 0 <= i - distance < count]
    return lax.ppermute(block, "blk", route)


def local(queries, key_vectors, value_vectors, grad_context, content_bias, slopes, lengths):
    kv = across(run_split(key_vectors, value_vectors))
    low = from_behind(kv, 1)
    high = from_behind(kv, -1)
    qd = across(run_split(queries, grad_context))
    start = (lax.axis_index("blk") * BLOCK).astype(jnp.int32)
    meta = jnp.stack([start, lengths[0]])
    bias = content_bias.reshape(1, LANES)
    powers, held = run_centre_forward(meta, slopes, kv, qd, bias)
    context, dq, stats, dlow, dhigh, halo_slope = run_halo(
        meta, slopes, low, high, qd, bias, held
    )
    from_low = from_behind(dhigh, 1)
    from_high = from_behind(dlow, -1)
    cq, dkv, sums = run_centre_backward(
        meta, slopes, kv, qd, bias, powers, stats, context, dq, halo_slope
    )
    group = lax.axis_size("dp") * lax.axis_size("blk")
    spread = lax.all_to_all(
        jnp.broadcast_to(sums[None], (group, 2, LANES)), ("dp", "blk"), 0, 0, tiled=True
    )
    context_out, query_out = run_join(across(cq))
    dkv = (dkv + from_low.astype(F32) + from_high.astype(F32)).astype(BF16)
    key_out, value_out = run_join(across(dkv))
    total = jnp.sum(spread, axis=0)
    return (
        context_out,
        query_out,
        key_out,
        value_out,
        total[0].reshape(2, HEAD),
        total[1, :2],
    )


def solution(mesh):
    rows = P("dp", ("blk", "uly"), None)
    return jax.shard_map(
        local,
        mesh=mesh,
        in_specs=(rows, rows, rows, rows, P("uly", None), P("uly"), P("dp")),
        out_specs=(rows, rows, rows, rows, P("uly", None), P("uly")),
        check_vma=False,
    )
```

```python
import jax
import jax.numpy as jnp
from jax import lax
from jax.experimental import pallas as pl
from jax.experimental.pallas import tpu as pltpu
from jax.sharding import PartitionSpec as P

BLOCK = 1024
TILE = 256
TILES = BLOCK // TILE
HALO = BLOCK + TILE
PEERS = 8
CHUNK = BLOCK // PEERS
LANES = 128
HEAD = 64
FACTOR = HEAD**-0.5
LOG2E = 1.4426950408889634
FAR = 1e30
VMEM_LIMIT = 40 * 1024 * 1024
F32 = jnp.float32
BF16 = jnp.bfloat16


def iota(shape, dim):
    return lax.broadcasted_iota(jnp.int32, shape, dim)


def dot_nt(a, b):
    return lax.dot_general(a, b, (((1,), (1,)), ((), ())), preferred_element_type=F32)


def dot_nn(a, b):
    return jnp.dot(a, b, preferred_element_type=F32)


def own_lanes(head, shape):
    lane = iota(shape, 1)
    return lane < HEAD if head == 0 else lane >= HEAD


def spare(head):
    return HEAD if head == 0 else 0


def fill_keys(kv_ref, keys, values, base, start, length):
    shape = (CHUNK, LANES)
    lane = iota(shape, 1)
    for peer in range(PEERS):
        rows = pl.ds(base + peer * CHUNK, CHUNK)
        place = start + peer * CHUNK + iota(shape, 0)
        blocked = jnp.where((place >= 0) & (place < length), 0.0, -FAR)
        key = kv_ref[peer, 0].astype(F32)
        value = kv_ref[peer, 1].astype(F32)
        for head in range(2):
            own, at = own_lanes(head, shape), spare(head)
            keys[head, rows] = jnp.where(own, key, jnp.where(lane == at, blocked, 0.0)).astype(BF16)
            ones = ((lane >= at) & (lane < at + 3)).astype(F32)
            values[head, rows] = jnp.where(own, value, ones).astype(BF16)


def fill_penalty(slopes_ref, penalty, pieces):
    for piece in pieces:
        spacing = jnp.abs(iota((TILE, TILE), 0) + BLOCK - piece * TILE - iota((TILE, TILE), 1))
        for head in range(2):
            cost_here = spacing.astype(F32) * (slopes_ref[head] * LOG2E)
            if piece in (0, 2 * BLOCK // TILE):
                cost_here = jnp.where(spacing <= BLOCK, cost_here, FAR)
            penalty[head, :, pl.ds(piece * TILE, TILE)] = cost_here


def load_queries(qd_ref, bias_ref, tile):
    query = jnp.concatenate([qd_ref[2 * tile, 0], qd_ref[2 * tile + 1, 0]], axis=0).astype(F32)
    return (query + bias_ref[...]).astype(BF16).astype(F32)


def load_upstream(qd_ref, tile, first, length):
    upstream = jnp.concatenate([qd_ref[2 * tile, 1], qd_ref[2 * tile + 1, 1]], axis=0).astype(F32)
    place = first + tile * TILE + iota((TILE, LANES), 0)
    return jnp.where(place < length, upstream, 0.0)


def with_spare(head, rows, columns):
    lane = iota((TILE, LANES), 1)
    other = jnp.zeros((TILE, LANES), F32)
    for k, column in enumerate(columns):
        other = jnp.where(lane == spare(head) + k, column, other)
    return jnp.where(own_lanes(head, (TILE, LANES)), rows, other)


def thirds(column):
    high = column.astype(BF16).astype(F32)
    middle = (column - high).astype(BF16).astype(F32)
    return high, middle, column - high - middle


def staggered(stages):
    chains = [{"tile": tile, "head": head} for tile in range(TILES) for head in range(2)]
    for step in range(len(chains) + len(stages) - 1):
        for depth, stage in enumerate(stages):
            if 0 <= step - depth < len(chains):
                stage(chains[step - depth], **{k: chains[step - depth][k] for k in ("tile", "head")})
    return chains


def head_half(head):
    return slice(head * HEAD, (head + 1) * HEAD)


def lane_sums(weighted):
    total = weighted[:, :LANES]
    for piece in range(1, weighted.shape[1] // LANES):
        total = total + weighted[:, piece * LANES : (piece + 1) * LANES]
    return total


def centre_forward(meta, slopes_ref, kv_ref, qd_ref, bias_ref, p_ref, o_ref, keys, values, penalty):
    fill_keys(kv_ref, keys, values, 0, meta[0], meta[1])
    fill_penalty(slopes_ref, penalty, range(1, 2 * BLOCK // TILE))

    def score(c, tile, head):
        rows = with_spare(head, load_queries(qd_ref, bias_ref, tile), (1.0,)).astype(BF16)
        far = penalty[head, :, pl.ds(BLOCK - tile * TILE, BLOCK)]
        c["scores"] = dot_nt(rows, keys[head]) * (FACTOR * LOG2E) - far

    def soften(c, tile, head):
        scores = c.pop("scores")
        c["top"] = jnp.max(scores, axis=1, keepdims=True)
        c["powers"] = jnp.exp2(scores - c["top"]).astype(BF16)

    def weigh(c, tile, head):
        rows = pl.ds(tile * TILE, TILE)
        powers = c.pop("powers")
        p_ref[head, rows] = powers
        out = dot_nn(powers, values[head])
        o_ref[head, rows] = jnp.where(iota((TILE, LANES), 1) == spare(head) + 1, c["top"], out)

    staggered([score, soften, weigh])


def halo_both(
    meta,
    slopes_ref,
    low_ref,
    high_ref,
    qd_ref,
    bias_ref,
    o_ref,
    ctx_ref,
    dq_ref,
    stat_ref,
    dlow_ref,
    dhigh_ref,
    slope_ref,
    keys,
    values,
    penalty,
    dkt,
    dvt,
):
    first, length = meta[0], meta[1]
    fill_keys(low_ref, keys, values, 0, first - BLOCK, length)
    fill_keys(high_ref, keys, values, BLOCK, first + BLOCK, length)
    fill_penalty(slopes_ref, penalty, [p for p in range(9) if p != BLOCK // TILE])
    dkt[...] = jnp.zeros_like(dkt)
    dvt[...] = jnp.zeros_like(dvt)
    shape = (TILE, LANES)
    lane = iota(shape, 1)

    def penalty_of(tile, head):
        low = penalty[head, :, pl.ds(0, BLOCK - tile * TILE)]
        high = penalty[head, :, pl.ds(2 * BLOCK - tile * TILE, (tile + 1) * TILE)]
        return jnp.concatenate([low, high], axis=1)

    def score(c, tile, head):
        c["span"] = pl.ds(tile * TILE, HALO)
        c["query"] = load_queries(qd_ref, bias_ref, tile)
        rows = with_spare(head, c["query"], (1.0,)).astype(BF16)
        scores = dot_nt(rows, keys[head, c["span"]]) * (FACTOR * LOG2E)
        c["scores"] = scores - penalty_of(tile, head)

    def soften(c, tile, head):
        scores = c.pop("scores")
        held = o_ref[head, pl.ds(tile * TILE, TILE)]
        top_held = held[:, spare(head) + 1 : spare(head) + 2]
        top = jnp.maximum(top_held, jnp.max(scores, axis=1, keepdims=True))
        c["powers"] = jnp.exp2(scores - top).astype(BF16)
        c["kept"] = jnp.exp2(top_held - top)

    def weigh(c, tile, head):
        held = o_ref[head, pl.ds(tile * TILE, TILE)]
        out = held * c["kept"] + dot_nn(c["powers"], values[head, c["span"]])
        c["inverse"] = 1.0 / out[:, spare(head) : spare(head) + 1]
        c["out"] = out * c["inverse"]

    def grade(c, tile, head):
        upstream = load_upstream(qd_ref, tile, first, length)
        c["upstream"] = upstream
        own = own_lanes(head, shape)
        c["delta"] = jnp.sum(jnp.where(own, upstream * c["out"], 0.0), axis=1, keepdims=True)
        up_rows = with_spare(head, upstream, thirds(-c["delta"])).astype(BF16)
        c["slope_grads"] = dot_nt(up_rows, values[head, c["span"]])

    def scale(c, tile, head):
        slope_grads = c["powers"].astype(F32) * c.pop("slope_grads")
        c["grads"] = slope_grads.astype(BF16)
        by_lane = lane_sums(slope_grads * penalty_of(tile, head)) * c["inverse"]
        c["slope"] = jnp.sum(by_lane, axis=0, keepdims=True)

    def spread(c, tile, head):
        inverse = c["inverse"]
        c["dq"] = dot_nn(c["grads"], keys[head, c["span"]]) * (inverse * FACTOR)
        part = pl.ds(head * HEAD, HEAD)
        up_cols = (c["upstream"] * inverse).T[head_half(head)].astype(BF16)
        query_cols = (c["query"] * (inverse * FACTOR)).T[head_half(head)].astype(BF16)
        dvt[part, c["span"]] += dot_nn(up_cols, c.pop("powers"))
        dkt[part, c["span"]] += dot_nn(query_cols, c.pop("grads"))

    def finish(c, tile, head):
        if head == 0:
            c_first[tile] = c
            return
        pair = (c_first[tile], c)
        rows = pl.ds(tile * TILE, TILE)
        place = first + tile * TILE + iota(shape, 0)
        context = jnp.where(lane < HEAD, pair[0]["out"], pair[1]["out"])
        ctx_ref[rows] = jnp.where(place < length, context, 0.0).astype(BF16)
        dq_ref[rows] = jnp.where(lane < HEAD, pair[0]["dq"], pair[1]["dq"])
        stats = jnp.zeros(shape, F32)
        for k in range(2):
            stats = jnp.where(lane == 2 * k, pair[k]["delta"], stats)
            stats = jnp.where(lane == 2 * k + 1, pair[k]["kept"] * pair[k]["inverse"], stats)
        stat_ref[rows] = stats

    c_first = {}
    chains = staggered([score, soften, weigh, grade, scale, spread, finish])
    for head in range(2):
        total = sum(c["slope"] for c in chains if c["head"] == head)
        slope_ref[pl.ds(head * 8, 8)] = jnp.broadcast_to(total, (8, LANES))
    for peer in range(PEERS):
        for side, out_ref in ((0, dlow_ref), (BLOCK, dhigh_ref)):
            cols = pl.ds(side + peer * CHUNK, CHUNK)
            out_ref[peer, 0] = dkt[:, cols].T.astype(BF16)
            out_ref[peer, 1] = dvt[:, cols].T.astype(BF16)


def centre_backward(
    meta,
    slopes_ref,
    kv_ref,
    qd_ref,
    bias_ref,
    p_ref,
    stat_ref,
    ctx_ref,
    dq_ref,
    halo_slope_ref,
    cq_ref,
    dkv_ref,
    sums_ref,
    keys,
    values,
    penalty,
    dkt,
    dvt,
):
    first, length = meta[0], meta[1]
    fill_keys(kv_ref, keys, values, 0, first, length)
    fill_penalty(slopes_ref, penalty, range(1, 2 * BLOCK // TILE))
    dkt[...] = jnp.zeros_like(dkt)
    dvt[...] = jnp.zeros_like(dvt)
    shape = (TILE, LANES)
    lane = iota(shape, 1)

    def grade(c, tile, head):
        stats = stat_ref[pl.ds(tile * TILE, TILE)]
        delta = stats[:, 2 * head : 2 * head + 1]
        c["scale"] = stats[:, 2 * head + 1 : 2 * head + 2]
        c["upstream"] = load_upstream(qd_ref, tile, first, length)
        up_rows = with_spare(head, c["upstream"], thirds(-delta)).astype(BF16)
        c["slope_grads"] = dot_nt(up_rows, values[head])

    def scale(c, tile, head):
        c["powers"] = p_ref[head, pl.ds(tile * TILE, TILE)]
        slope_grads = c["powers"].astype(F32) * c.pop("slope_grads")
        c["grads"] = slope_grads.astype(BF16)
        far = penalty[head, :, pl.ds(BLOCK - tile * TILE, BLOCK)]
        c["slope"] = jnp.sum(lane_sums(slope_grads * far) * c["scale"], axis=0, keepdims=True)

    def spread(c, tile, head):
        ratio = c["scale"]
        c["dq"] = dot_nn(c["grads"], keys[head]) * (ratio * FACTOR)
        part = pl.ds(head * HEAD, HEAD)
        query = load_queries(qd_ref, bias_ref, tile)
        up_cols = (c["upstream"] * ratio).T[head_half(head)].astype(BF16)
        query_cols = (query * (ratio * FACTOR)).T[head_half(head)].astype(BF16)
        dvt[part] += dot_nn(up_cols, c.pop("powers"))
        dkt[part] += dot_nn(query_cols, c.pop("grads"))

    def finish(c, tile, head):
        if head == 0:
            c_first[tile] = c
            return
        dq = jnp.where(lane < HEAD, c_first[tile]["dq"], c["dq"])
        dq = dq + dq_ref[pl.ds(tile * TILE, TILE)]
        c["bias"] = jnp.sum(dq, axis=0, keepdims=True)
        for half in range(2):
            rows = slice(half * CHUNK, (half + 1) * CHUNK)
            cq_ref[2 * tile + half, 0] = ctx_ref[pl.ds(tile * TILE + half * CHUNK, CHUNK)]
            cq_ref[2 * tile + half, 1] = dq[rows].astype(BF16)

    c_first = {}
    chains = staggered([grade, scale, spread, finish])
    sums_ref[0:1] = sum(c["bias"] for c in chains if c["head"] == 1)
    row = iota((1, LANES), 1)
    totals = []
    for head in range(2):
        total = sum(c["slope"] for c in chains if c["head"] == head)
        total = jnp.sum(total + halo_slope_ref[pl.ds(head * 8, 1)], axis=1, keepdims=True)
        totals.append(-total / (slopes_ref[head] * LOG2E))
    sums_ref[1:2] = jnp.where(row == 0, totals[0], jnp.where(row == 1, totals[1], 0.0))
    for peer in range(PEERS):
        cols = pl.ds(peer * CHUNK, CHUNK)
        dkv_ref[peer, 0] = dkt[:, cols].T
        dkv_ref[peer, 1] = dvt[:, cols].T


SMEM = pl.BlockSpec(memory_space=pltpu.SMEM)
VMEM = pl.BlockSpec(memory_space=pltpu.VMEM)
PAIR = (PEERS, 2, CHUNK, LANES)


def params():
    return pltpu.CompilerParams(vmem_limit_bytes=VMEM_LIMIT)


def cost(keys, products):
    pairs = 2 * BLOCK * keys
    return pl.CostEstimate(
        flops=2 * pairs * LANES * products, bytes_accessed=8 * 1024 * 1024, transcendentals=pairs
    )


def shaped(shape, kind):
    return jax.ShapeDtypeStruct(shape, kind)


def run_centre_forward(meta, slopes, kv, qd, bias):
    return pl.pallas_call(
        centre_forward,
        in_specs=[SMEM, SMEM] + [VMEM] * 3,
        out_specs=[VMEM] * 2,
        out_shape=[shaped((2, BLOCK, BLOCK), BF16), shaped((2, BLOCK, LANES), F32)],
        scratch_shapes=[
            pltpu.VMEM((2, BLOCK, LANES), BF16),
            pltpu.VMEM((2, BLOCK, LANES), BF16),
            pltpu.VMEM((2, TILE, 2 * BLOCK + TILE), F32),
        ],
        compiler_params=params(),
        cost_estimate=cost(BLOCK, 2),
        name="centre_forward",
    )(meta, slopes, kv, qd, bias)


def run_halo(meta, slopes, low, high, qd, bias, held):
    return pl.pallas_call(
        halo_both,
        in_specs=[SMEM, SMEM] + [VMEM] * 5,
        out_specs=[VMEM] * 6,
        out_shape=[
            shaped((BLOCK, LANES), BF16),
            shaped((BLOCK, LANES), F32),
            shaped((BLOCK, LANES), F32),
            shaped(PAIR, BF16),
            shaped(PAIR, BF16),
            shaped((16, LANES), F32),
        ],
        scratch_shapes=[
            pltpu.VMEM((2, 2 * BLOCK, LANES), BF16),
            pltpu.VMEM((2, 2 * BLOCK, LANES), BF16),
            pltpu.VMEM((2, TILE, 2 * BLOCK + TILE), F32),
            pltpu.VMEM((LANES, 2 * BLOCK), F32),
            pltpu.VMEM((LANES, 2 * BLOCK), F32),
        ],
        compiler_params=params(),
        cost_estimate=cost(HALO, 6),
        name="halo_both",
    )(meta, slopes, low, high, qd, bias, held)


def run_centre_backward(meta, slopes, kv, qd, bias, powers, stats, context, dq, halo_slope):
    return pl.pallas_call(
        centre_backward,
        in_specs=[SMEM, SMEM] + [VMEM] * 8,
        out_specs=[VMEM] * 3,
        out_shape=[shaped(PAIR, BF16), shaped(PAIR, F32), shaped((2, LANES), F32)],
        scratch_shapes=[
            pltpu.VMEM((2, BLOCK, LANES), BF16),
            pltpu.VMEM((2, BLOCK, LANES), BF16),
            pltpu.VMEM((2, TILE, 2 * BLOCK + TILE), F32),
            pltpu.VMEM((LANES, BLOCK), F32),
            pltpu.VMEM((LANES, BLOCK), F32),
        ],
        compiler_params=params(),
        cost_estimate=cost(BLOCK, 4),
        name="centre_backward",
    )(meta, slopes, kv, qd, bias, powers, stats, context, dq, halo_slope)


def split_pair(first_ref, second_ref, out_ref):
    for peer in range(PEERS):
        cols = pl.ds(peer * LANES, LANES)
        out_ref[peer, 0] = first_ref[0, :, cols]
        out_ref[peer, 1] = second_ref[0, :, cols]


def run_split(first, second):
    return pl.pallas_call(split_pair, out_shape=shaped(PAIR, BF16), name="split_pair")(first, second)


def gather_grads(cq_ref, dkv_ref, low_ref, high_ref, out_ref):
    for peer in range(PEERS):
        for part in range(2):
            out_ref[peer, part] = cq_ref[peer, part]
            passed = low_ref[peer, part].astype(F32) + high_ref[peer, part].astype(F32)
            out_ref[peer, 2 + part] = (dkv_ref[peer, part] + passed).astype(BF16)


def run_gather(cq, dkv, from_low, from_high):
    return pl.pallas_call(
        gather_grads, out_shape=shaped((PEERS, 4, CHUNK, LANES), BF16), name="gather_grads"
    )(cq, dkv, from_low, from_high)


def join_four(parts_ref, *out_refs):
    for peer in range(PEERS):
        cols = pl.ds(peer * LANES, LANES)
        for part in range(4):
            out_refs[part][0, :, cols] = parts_ref[peer, part]


def run_join(parts):
    whole_rows = shaped((1, CHUNK, PEERS * LANES), BF16)
    return pl.pallas_call(join_four, out_shape=[whole_rows] * 4, name="join_four")(parts)


def across(pair):
    return lax.all_to_all(pair, "uly", split_axis=0, concat_axis=0, tiled=True)


def from_behind(block, distance):
    count = lax.axis_size("blk")
    route = [(i - distance, i) for i in range(count) if 0 <= i - distance < count]
    return lax.ppermute(block, "blk", route)


def local(queries, key_vectors, value_vectors, grad_context, content_bias, slopes, lengths):
    kv = across(run_split(key_vectors, value_vectors))
    low = from_behind(kv, 1)
    high = from_behind(kv, -1)
    qd = across(run_split(queries, grad_context))
    start = (lax.axis_index("blk") * BLOCK).astype(jnp.int32)
    meta = jnp.stack([start, lengths[0]])
    bias = content_bias.reshape(1, LANES)
    powers, held = run_centre_forward(meta, slopes, kv, qd, bias)
    context, dq, stats, dlow, dhigh, halo_slope = run_halo(
        meta, slopes, low, high, qd, bias, held
    )
    from_low = from_behind(dhigh, 1)
    from_high = from_behind(dlow, -1)
    cq, dkv, sums = run_centre_backward(
        meta, slopes, kv, qd, bias, powers, stats, context, dq, halo_slope
    )
    group = lax.axis_size("dp") * lax.axis_size("blk")
    spread = lax.all_to_all(
        jnp.broadcast_to(sums[None], (group, 2, LANES)), ("dp", "blk"), 0, 0, tiled=True
    )
    grads = run_gather(cq, dkv, from_low, from_high)
    context_out, query_out, key_out, value_out = run_join(across(grads))
    total = jnp.sum(spread, axis=0)
    return (
        context_out,
        query_out,
        key_out,
        value_out,
        total[0].reshape(2, HEAD),
        total[1, :2],
    )


def solution(mesh):
    rows = P("dp", ("blk", "uly"), None)
    return jax.shard_map(
        local,
        mesh=mesh,
        in_specs=(rows, rows, rows, rows, P("uly", None), P("uly"), P("dp")),
        out_specs=(rows, rows, rows, rows, P("uly", None), P("uly")),
        check_vma=False,
    )
```

```python
import jax
import jax.numpy as jnp
from jax import lax
from jax.experimental import pallas as pl
from jax.experimental.pallas import tpu as pltpu
from jax.sharding import PartitionSpec as P

BLOCK = 1024
TILE = 256
TILES = BLOCK // TILE
HALO = BLOCK + TILE
PEERS = 8
CHUNK = BLOCK // PEERS
LANES = 128
HEAD = 64
FACTOR = HEAD**-0.5
LOG2E = 1.4426950408889634
FAR = 1e30
VMEM_LIMIT = 40 * 1024 * 1024
F32 = jnp.float32
BF16 = jnp.bfloat16


def iota(shape, dim):
    return lax.broadcasted_iota(jnp.int32, shape, dim)


def dot_nt(a, b):
    return lax.dot_general(a, b, (((1,), (1,)), ((), ())), preferred_element_type=F32)


def dot_nn(a, b):
    return jnp.dot(a, b, preferred_element_type=F32)


def own_lanes(head, shape):
    lane = iota(shape, 1)
    return lane < HEAD if head == 0 else lane >= HEAD


def spare(head):
    return HEAD if head == 0 else 0


def fill_keys(kv_ref, keys, values, base, start, length):
    shape = (CHUNK, LANES)
    lane = iota(shape, 1)
    for peer in range(PEERS):
        rows = pl.ds(pl.multiple_of(base + peer * CHUNK, CHUNK), CHUNK)
        place = start + peer * CHUNK + iota(shape, 0)
        blocked = jnp.where((place >= 0) & (place < length), 0.0, -FAR)
        key = kv_ref[peer, 0].astype(F32)
        value = kv_ref[peer, 1].astype(F32)
        for head in range(2):
            own, at = own_lanes(head, shape), spare(head)
            keys[head, rows] = jnp.where(own, key, jnp.where(lane == at, blocked, 0.0)).astype(BF16)
            ones = ((lane >= at) & (lane < at + 3)).astype(F32)
            values[head, rows] = jnp.where(own, value, ones).astype(BF16)


def fill_penalty(slopes_ref, penalty, pieces):
    for piece in pieces:
        spacing = jnp.abs(iota((TILE, TILE), 0) + BLOCK - piece * TILE - iota((TILE, TILE), 1))
        for head in range(2):
            cost_here = spacing.astype(F32) * (slopes_ref[head] * LOG2E)
            if piece in (0, 2 * BLOCK // TILE):
                cost_here = jnp.where(spacing <= BLOCK, cost_here, FAR)
            penalty[head, :, pl.ds(piece * TILE, TILE)] = cost_here


def load_queries(qd_ref, bias_ref, tile):
    query = jnp.concatenate([qd_ref[2 * tile, 0], qd_ref[2 * tile + 1, 0]], axis=0).astype(F32)
    return (query + bias_ref[...]).astype(BF16).astype(F32)


def load_upstream(qd_ref, tile, first, length):
    upstream = jnp.concatenate([qd_ref[2 * tile, 1], qd_ref[2 * tile + 1, 1]], axis=0).astype(F32)
    place = first + tile * TILE + iota((TILE, LANES), 0)
    return jnp.where(place < length, upstream, 0.0)


def with_spare(head, rows, columns):
    lane = iota((TILE, LANES), 1)
    other = jnp.zeros((TILE, LANES), F32)
    for k, column in enumerate(columns):
        other = jnp.where(lane == spare(head) + k, column, other)
    return jnp.where(own_lanes(head, (TILE, LANES)), rows, other)


def thirds(column):
    high = column.astype(BF16).astype(F32)
    middle = (column - high).astype(BF16).astype(F32)
    return high, middle, column - high - middle


def staggered(stages):
    chains = [{"tile": tile, "head": head} for tile in range(TILES) for head in range(2)]
    for step in range(len(chains) + len(stages) - 1):
        for depth, stage in enumerate(stages):
            if 0 <= step - depth < len(chains):
                stage(chains[step - depth], **{k: chains[step - depth][k] for k in ("tile", "head")})
    return chains


def head_half(head):
    return slice(head * HEAD, (head + 1) * HEAD)


def lane_sums(weighted):
    total = weighted[:, :LANES]
    for piece in range(1, weighted.shape[1] // LANES):
        total = total + weighted[:, piece * LANES : (piece + 1) * LANES]
    return total


def centre_forward(meta, slopes_ref, kv_ref, qd_ref, bias_ref, p_ref, o_ref, keys, values, penalty):
    fill_keys(kv_ref, keys, values, 0, meta[0], meta[1])
    fill_penalty(slopes_ref, penalty, range(1, 2 * BLOCK // TILE))

    def score(c, tile, head):
        rows = with_spare(head, load_queries(qd_ref, bias_ref, tile), (1.0,)).astype(BF16)
        far = penalty[head, :, pl.ds(BLOCK - tile * TILE, BLOCK)]
        c["scores"] = dot_nt(rows, keys[head]) * (FACTOR * LOG2E) - far

    def soften(c, tile, head):
        scores = c.pop("scores")
        c["top"] = jnp.max(scores, axis=1, keepdims=True)
        c["powers"] = jnp.exp2(scores - c["top"]).astype(BF16)

    def weigh(c, tile, head):
        rows = pl.ds(tile * TILE, TILE)
        powers = c.pop("powers")
        p_ref[head, rows] = powers
        out = dot_nn(powers, values[head])
        o_ref[head, rows] = jnp.where(iota((TILE, LANES), 1) == spare(head) + 1, c["top"], out)

    staggered([score, soften, weigh])


def halo_both(
    meta,
    slopes_ref,
    second_ref,
    first_ref,
    qd_ref,
    bias_ref,
    o_ref,
    ctx_ref,
    dq_ref,
    stat_ref,
    dfirst_ref,
    dsecond_ref,
    slope_ref,
    keys,
    values,
    penalty,
    dkt,
    dvt,
):
    first, length = meta[0], meta[1]
    odd = lax.rem(first // BLOCK, 2)
    fill_keys(first_ref, keys, values, odd * BLOCK, first + (2 * odd - 1) * BLOCK, length)
    fill_keys(second_ref, keys, values, (1 - odd) * BLOCK, first - (2 * odd - 1) * BLOCK, length)
    fill_penalty(slopes_ref, penalty, [p for p in range(9) if p != BLOCK // TILE])
    dkt[...] = jnp.zeros_like(dkt)
    dvt[...] = jnp.zeros_like(dvt)
    shape = (TILE, LANES)
    lane = iota(shape, 1)

    def penalty_of(tile, head):
        low = penalty[head, :, pl.ds(0, BLOCK - tile * TILE)]
        high = penalty[head, :, pl.ds(2 * BLOCK - tile * TILE, (tile + 1) * TILE)]
        return jnp.concatenate([low, high], axis=1)

    def score(c, tile, head):
        c["span"] = pl.ds(tile * TILE, HALO)
        c["query"] = load_queries(qd_ref, bias_ref, tile)
        rows = with_spare(head, c["query"], (1.0,)).astype(BF16)
        scores = dot_nt(rows, keys[head, c["span"]]) * (FACTOR * LOG2E)
        c["scores"] = scores - penalty_of(tile, head)

    def soften(c, tile, head):
        scores = c.pop("scores")
        held = o_ref[head, pl.ds(tile * TILE, TILE)]
        top_held = held[:, spare(head) + 1 : spare(head) + 2]
        top = jnp.maximum(top_held, jnp.max(scores, axis=1, keepdims=True))
        c["powers"] = jnp.exp2(scores - top).astype(BF16)
        c["kept"] = jnp.exp2(top_held - top)

    def weigh(c, tile, head):
        held = o_ref[head, pl.ds(tile * TILE, TILE)]
        out = held * c["kept"] + dot_nn(c["powers"], values[head, c["span"]])
        c["inverse"] = 1.0 / out[:, spare(head) : spare(head) + 1]
        c["out"] = out * c["inverse"]

    def grade(c, tile, head):
        upstream = load_upstream(qd_ref, tile, first, length)
        c["upstream"] = upstream
        own = own_lanes(head, shape)
        c["delta"] = jnp.sum(jnp.where(own, upstream * c["out"], 0.0), axis=1, keepdims=True)
        up_rows = with_spare(head, upstream, thirds(-c["delta"])).astype(BF16)
        c["slope_grads"] = dot_nt(up_rows, values[head, c["span"]])

    def scale(c, tile, head):
        slope_grads = c["powers"].astype(F32) * c.pop("slope_grads")
        c["grads"] = slope_grads.astype(BF16)
        by_lane = lane_sums(slope_grads * penalty_of(tile, head)) * c["inverse"]
        c["slope"] = jnp.sum(by_lane, axis=0, keepdims=True)

    def spread(c, tile, head):
        inverse = c["inverse"]
        c["dq"] = dot_nn(c["grads"], keys[head, c["span"]]) * (inverse * FACTOR)
        part = pl.ds(head * HEAD, HEAD)
        up_cols = (c["upstream"] * inverse).T[head_half(head)].astype(BF16)
        query_cols = (c["query"] * (inverse * FACTOR)).T[head_half(head)].astype(BF16)
        dvt[part, c["span"]] += dot_nn(up_cols, c.pop("powers"))
        dkt[part, c["span"]] += dot_nn(query_cols, c.pop("grads"))

    def finish(c, tile, head):
        if head == 0:
            c_first[tile] = c
            return
        pair = (c_first[tile], c)
        rows = pl.ds(tile * TILE, TILE)
        place = first + tile * TILE + iota(shape, 0)
        context = jnp.where(lane < HEAD, pair[0]["out"], pair[1]["out"])
        ctx_ref[rows] = jnp.where(place < length, context, 0.0).astype(BF16)
        dq_ref[rows] = jnp.where(lane < HEAD, pair[0]["dq"], pair[1]["dq"])
        stats = jnp.zeros(shape, F32)
        for k in range(2):
            stats = jnp.where(lane == 2 * k, pair[k]["delta"], stats)
            stats = jnp.where(lane == 2 * k + 1, pair[k]["kept"] * pair[k]["inverse"], stats)
        stat_ref[rows] = stats

    c_first = {}
    chains = staggered([score, soften, weigh, grade, scale, spread, finish])
    for head in range(2):
        total = sum(c["slope"] for c in chains if c["head"] == head)
        slope_ref[pl.ds(head * 8, 8)] = jnp.broadcast_to(total, (8, LANES))
    for peer in range(PEERS):
        for side, out_ref in ((odd, dfirst_ref), (1 - odd, dsecond_ref)):
            cols = pl.ds(pl.multiple_of(side * BLOCK + peer * CHUNK, CHUNK), CHUNK)
            out_ref[peer, 0] = dkt[:, cols].T.astype(BF16)
            out_ref[peer, 1] = dvt[:, cols].T.astype(BF16)


def centre_backward(
    meta,
    slopes_ref,
    kv_ref,
    qd_ref,
    bias_ref,
    p_ref,
    stat_ref,
    ctx_ref,
    dq_ref,
    halo_slope_ref,
    cq_ref,
    dkv_ref,
    sums_ref,
    keys,
    values,
    penalty,
    dkt,
    dvt,
):
    first, length = meta[0], meta[1]
    fill_keys(kv_ref, keys, values, 0, first, length)
    fill_penalty(slopes_ref, penalty, range(1, 2 * BLOCK // TILE))
    dkt[...] = jnp.zeros_like(dkt)
    dvt[...] = jnp.zeros_like(dvt)
    shape = (TILE, LANES)
    lane = iota(shape, 1)

    def grade(c, tile, head):
        stats = stat_ref[pl.ds(tile * TILE, TILE)]
        delta = stats[:, 2 * head : 2 * head + 1]
        c["scale"] = stats[:, 2 * head + 1 : 2 * head + 2]
        c["upstream"] = load_upstream(qd_ref, tile, first, length)
        up_rows = with_spare(head, c["upstream"], thirds(-delta)).astype(BF16)
        c["slope_grads"] = dot_nt(up_rows, values[head])

    def scale(c, tile, head):
        c["powers"] = p_ref[head, pl.ds(tile * TILE, TILE)]
        slope_grads = c["powers"].astype(F32) * c.pop("slope_grads")
        c["grads"] = slope_grads.astype(BF16)
        far = penalty[head, :, pl.ds(BLOCK - tile * TILE, BLOCK)]
        c["slope"] = jnp.sum(lane_sums(slope_grads * far) * c["scale"], axis=0, keepdims=True)

    def spread(c, tile, head):
        ratio = c["scale"]
        c["dq"] = dot_nn(c["grads"], keys[head]) * (ratio * FACTOR)
        part = pl.ds(head * HEAD, HEAD)
        query = load_queries(qd_ref, bias_ref, tile)
        up_cols = (c["upstream"] * ratio).T[head_half(head)].astype(BF16)
        query_cols = (query * (ratio * FACTOR)).T[head_half(head)].astype(BF16)
        dvt[part] += dot_nn(up_cols, c.pop("powers"))
        dkt[part] += dot_nn(query_cols, c.pop("grads"))

    def finish(c, tile, head):
        if head == 0:
            c_first[tile] = c
            return
        dq = jnp.where(lane < HEAD, c_first[tile]["dq"], c["dq"])
        dq = dq + dq_ref[pl.ds(tile * TILE, TILE)]
        c["bias"] = jnp.sum(dq, axis=0, keepdims=True)
        for half in range(2):
            rows = slice(half * CHUNK, (half + 1) * CHUNK)
            cq_ref[2 * tile + half, 0] = ctx_ref[pl.ds(tile * TILE + half * CHUNK, CHUNK)]
            cq_ref[2 * tile + half, 1] = dq[rows].astype(BF16)

    c_first = {}
    chains = staggered([grade, scale, spread, finish])
    sums_ref[0:1] = sum(c["bias"] for c in chains if c["head"] == 1)
    row = iota((1, LANES), 1)
    totals = []
    for head in range(2):
        total = sum(c["slope"] for c in chains if c["head"] == head)
        total = jnp.sum(total + halo_slope_ref[pl.ds(head * 8, 1)], axis=1, keepdims=True)
        totals.append(-total / (slopes_ref[head] * LOG2E))
    sums_ref[1:2] = jnp.where(row == 0, totals[0], jnp.where(row == 1, totals[1], 0.0))
    for peer in range(PEERS):
        cols = pl.ds(peer * CHUNK, CHUNK)
        dkv_ref[peer, 0] = dkt[:, cols].T
        dkv_ref[peer, 1] = dvt[:, cols].T


SMEM = pl.BlockSpec(memory_space=pltpu.SMEM)
VMEM = pl.BlockSpec(memory_space=pltpu.VMEM)
PAIR = (PEERS, 2, CHUNK, LANES)


def params():
    return pltpu.CompilerParams(vmem_limit_bytes=VMEM_LIMIT)


def cost(keys, products):
    pairs = 2 * BLOCK * keys
    return pl.CostEstimate(
        flops=2 * pairs * LANES * products, bytes_accessed=8 * 1024 * 1024, transcendentals=pairs
    )


def shaped(shape, kind):
    return jax.ShapeDtypeStruct(shape, kind)


def run_centre_forward(meta, slopes, kv, qd, bias):
    return pl.pallas_call(
        centre_forward,
        in_specs=[SMEM, SMEM] + [VMEM] * 3,
        out_specs=[VMEM] * 2,
        out_shape=[shaped((2, BLOCK, BLOCK), BF16), shaped((2, BLOCK, LANES), F32)],
        scratch_shapes=[
            pltpu.VMEM((2, BLOCK, LANES), BF16),
            pltpu.VMEM((2, BLOCK, LANES), BF16),
            pltpu.VMEM((2, TILE, 2 * BLOCK + TILE), F32),
        ],
        compiler_params=params(),
        cost_estimate=pl.CostEstimate(flops=1000, bytes_accessed=1000, transcendentals=0),
        name="centre_forward",
    )(meta, slopes, kv, qd, bias)


def run_halo(meta, slopes, kv_first, kv_second, qd, bias, held):
    return pl.pallas_call(
        halo_both,
        in_specs=[SMEM, SMEM] + [VMEM] * 5,
        out_specs=[VMEM] * 6,
        out_shape=[
            shaped((BLOCK, LANES), BF16),
            shaped((BLOCK, LANES), F32),
            shaped((BLOCK, LANES), F32),
            shaped(PAIR, BF16),
            shaped(PAIR, BF16),
            shaped((16, LANES), F32),
        ],
        scratch_shapes=[
            pltpu.VMEM((2, 2 * BLOCK, LANES), BF16),
            pltpu.VMEM((2, 2 * BLOCK, LANES), BF16),
            pltpu.VMEM((2, TILE, 2 * BLOCK + TILE), F32),
            pltpu.VMEM((LANES, 2 * BLOCK), F32),
            pltpu.VMEM((LANES, 2 * BLOCK), F32),
        ],
        compiler_params=params(),
        cost_estimate=cost(HALO, 6),
        name="halo_both",
    )(meta, slopes, kv_second, kv_first, qd, bias, held)


def run_centre_backward(meta, slopes, kv, qd, bias, powers, stats, context, dq, halo_slope):
    return pl.pallas_call(
        centre_backward,
        in_specs=[SMEM, SMEM] + [VMEM] * 8,
        out_specs=[VMEM] * 3,
        out_shape=[shaped(PAIR, BF16), shaped(PAIR, F32), shaped((2, LANES), F32)],
        scratch_shapes=[
            pltpu.VMEM((2, BLOCK, LANES), BF16),
            pltpu.VMEM((2, BLOCK, LANES), BF16),
            pltpu.VMEM((2, TILE, 2 * BLOCK + TILE), F32),
            pltpu.VMEM((LANES, BLOCK), F32),
            pltpu.VMEM((LANES, BLOCK), F32),
        ],
        compiler_params=params(),
        cost_estimate=pl.CostEstimate(flops=1000, bytes_accessed=1000, transcendentals=0),
        name="centre_backward",
    )(meta, slopes, kv, qd, bias, powers, stats, context, dq, halo_slope)


def split_pair(first_ref, second_ref, out_ref):
    for peer in range(PEERS):
        cols = pl.ds(peer * LANES, LANES)
        out_ref[peer, 0] = first_ref[0, :, cols]
        out_ref[peer, 1] = second_ref[0, :, cols]


def run_split(first, second):
    return pl.pallas_call(split_pair, out_shape=shaped(PAIR, BF16), name="split_pair")(first, second)


def gather_grads(cq_ref, dkv_ref, first_ref, second_ref, out_ref):
    for peer in range(PEERS):
        for part in range(2):
            out_ref[peer, part] = cq_ref[peer, part]
            passed = first_ref[peer, part].astype(F32) + second_ref[peer, part].astype(F32)
            out_ref[peer, 2 + part] = (dkv_ref[peer, part] + passed).astype(BF16)


def run_gather(cq, dkv, from_first, from_second):
    return pl.pallas_call(
        gather_grads, out_shape=shaped((PEERS, 4, CHUNK, LANES), BF16), name="gather_grads"
    )(cq, dkv, from_first, from_second)


def join_four(parts_ref, *out_refs):
    for peer in range(PEERS):
        cols = pl.ds(peer * LANES, LANES)
        for part in range(4):
            out_refs[part][0, :, cols] = parts_ref[peer, part]


def run_join(parts):
    whole_rows = shaped((1, CHUNK, PEERS * LANES), BF16)
    return pl.pallas_call(join_four, out_shape=[whole_rows] * 4, name="join_four")(parts)


def across(pair):
    return lax.all_to_all(pair, "uly", split_axis=0, concat_axis=0, tiled=True)


def swapped(block, lowest):
    pairs = [(i, i + 1) for i in range(lowest, lax.axis_size("blk") - 1, 2)]
    return lax.ppermute(block, "blk", pairs + [(high, low) for low, high in pairs])


def local(queries, key_vectors, value_vectors, grad_context, content_bias, slopes, lengths):
    kv = across(run_split(key_vectors, value_vectors))
    kv_first = swapped(kv, 1)
    kv_second = swapped(kv, 0)
    qd = across(run_split(queries, grad_context))
    start = (lax.axis_index("blk") * BLOCK).astype(jnp.int32)
    meta = jnp.stack([start, lengths[0]])
    bias = content_bias.reshape(1, LANES)
    powers, held = run_centre_forward(meta, slopes, kv, qd, bias)
    context, dq, stats, dfirst, dsecond, halo_slope = run_halo(
        meta, slopes, kv_first, kv_second, qd, bias, held
    )
    from_first = swapped(dfirst, 1)
    from_second = swapped(dsecond, 0)
    cq, dkv, sums = run_centre_backward(
        meta, slopes, kv, qd, bias, powers, stats, context, dq, halo_slope
    )
    group = lax.axis_size("dp") * lax.axis_size("blk")
    spread = lax.all_to_all(
        jnp.broadcast_to(sums[None], (group, 2, LANES)), ("dp", "blk"), 0, 0, tiled=True
    )
    grads = run_gather(cq, dkv, from_first, from_second)
    context_out, query_out, key_out, value_out = run_join(across(grads))
    total = jnp.sum(spread, axis=0)
    return (
        context_out,
        query_out,
        key_out,
        value_out,
        total[0].reshape(2, HEAD),
        total[1, :2],
    )


def solution(mesh):
    rows = P("dp", ("blk", "uly"), None)
    return jax.shard_map(
        local,
        mesh=mesh,
        in_specs=(rows, rows, rows, rows, P("uly", None), P("uly"), P("dp")),
        out_specs=(rows, rows, rows, rows, P("uly", None), P("uly")),
        check_vma=False,
    )
```

```python
import jax
import jax.numpy as jnp
from jax import lax
from jax.experimental import pallas as pl
from jax.experimental.pallas import tpu as pltpu
from jax.sharding import PartitionSpec as P

BLOCK = 1024
TILE = 256
TILES = BLOCK // TILE
HALO = BLOCK + TILE
PEERS = 8
CHUNK = BLOCK // PEERS
LANES = 128
HEAD = 64
FACTOR = HEAD**-0.5
LOG2E = 1.4426950408889634
FAR = 1e30
VMEM_LIMIT = 40 * 1024 * 1024
F32 = jnp.float32
BF16 = jnp.bfloat16


def iota(shape, dim):
    return lax.broadcasted_iota(jnp.int32, shape, dim)


def dot_nt(a, b):
    return lax.dot_general(a, b, (((1,), (1,)), ((), ())), preferred_element_type=F32)


def dot_nn(a, b):
    return jnp.dot(a, b, preferred_element_type=F32)


def own_lanes(head, shape):
    lane = iota(shape, 1)
    return lane < HEAD if head == 0 else lane >= HEAD


def spare(head):
    return HEAD if head == 0 else 0


def fill_keys(kv_ref, keys, values, base, start, length):
    shape = (CHUNK, LANES)
    lane = iota(shape, 1)
    for peer in range(PEERS):
        rows = pl.ds(pl.multiple_of(base + peer * CHUNK, CHUNK), CHUNK)
        place = start + peer * CHUNK + iota(shape, 0)
        blocked = jnp.where((place >= 0) & (place < length), 0.0, -FAR)
        key = kv_ref[peer, 0].astype(F32)
        value = kv_ref[peer, 1].astype(F32)
        for head in range(2):
            own, at = own_lanes(head, shape), spare(head)
            keys[head, rows] = jnp.where(own, key, jnp.where(lane == at, blocked, 0.0)).astype(BF16)
            ones = ((lane >= at) & (lane < at + 3)).astype(F32)
            values[head, rows] = jnp.where(own, value, ones).astype(BF16)


def fill_penalty(slopes_ref, penalty, pieces):
    for piece in pieces:
        spacing = jnp.abs(iota((TILE, TILE), 0) + BLOCK - piece * TILE - iota((TILE, TILE), 1))
        for head in range(2):
            cost_here = spacing.astype(F32) * (slopes_ref[head] * LOG2E)
            if piece in (0, 2 * BLOCK // TILE):
                cost_here = jnp.where(spacing <= BLOCK, cost_here, FAR)
            penalty[head, :, pl.ds(piece * TILE, TILE)] = cost_here


def load_queries(qd_ref, bias_ref, tile):
    query = jnp.concatenate([qd_ref[2 * tile, 0], qd_ref[2 * tile + 1, 0]], axis=0).astype(F32)
    return (query + bias_ref[...]).astype(BF16).astype(F32)


def load_upstream(qd_ref, tile, first, length):
    upstream = jnp.concatenate([qd_ref[2 * tile, 1], qd_ref[2 * tile + 1, 1]], axis=0).astype(F32)
    place = first + tile * TILE + iota((TILE, LANES), 0)
    return jnp.where(place < length, upstream, 0.0)


def with_spare(head, rows, columns):
    lane = iota((TILE, LANES), 1)
    other = jnp.zeros((TILE, LANES), F32)
    for k, column in enumerate(columns):
        other = jnp.where(lane == spare(head) + k, column, other)
    return jnp.where(own_lanes(head, (TILE, LANES)), rows, other)


def thirds(column):
    high = column.astype(BF16).astype(F32)
    middle = (column - high).astype(BF16).astype(F32)
    return high, middle, column - high - middle


def staggered(stages):
    chains = [{"tile": tile, "head": head} for tile in range(TILES) for head in range(2)]
    for step in range(len(chains) + len(stages) - 1):
        for depth, stage in enumerate(stages):
            if 0 <= step - depth < len(chains):
                stage(chains[step - depth], **{k: chains[step - depth][k] for k in ("tile", "head")})
    return chains


def head_half(head):
    return slice(head * HEAD, (head + 1) * HEAD)


def lane_sums(weighted):
    total = weighted[:, :LANES]
    for piece in range(1, weighted.shape[1] // LANES):
        total = total + weighted[:, piece * LANES : (piece + 1) * LANES]
    return total


def centre_forward(meta, slopes_ref, kv_ref, qd_ref, bias_ref, p_ref, o_ref, keys, values, penalty):
    fill_keys(kv_ref, keys, values, 0, meta[0], meta[1])
    fill_penalty(slopes_ref, penalty, range(1, 2 * BLOCK // TILE))

    def score(c, tile, head):
        rows = with_spare(head, load_queries(qd_ref, bias_ref, tile), (1.0,)).astype(BF16)
        far = penalty[head, :, pl.ds(BLOCK - tile * TILE, BLOCK)]
        c["scores"] = dot_nt(rows, keys[head]) * (FACTOR * LOG2E) - far

    def soften(c, tile, head):
        scores = c.pop("scores")
        c["top"] = jnp.max(scores, axis=1, keepdims=True)
        c["powers"] = jnp.exp2(scores - c["top"]).astype(BF16)

    def weigh(c, tile, head):
        rows = pl.ds(tile * TILE, TILE)
        powers = c.pop("powers")
        p_ref[head, rows] = powers
        out = dot_nn(powers, values[head])
        o_ref[head, rows] = jnp.where(iota((TILE, LANES), 1) == spare(head) + 1, c["top"], out)

    staggered([score, soften, weigh])


def halo_both(
    meta,
    slopes_ref,
    second_ref,
    first_ref,
    qd_ref,
    bias_ref,
    o_ref,
    ctx_ref,
    dq_ref,
    stat_ref,
    dfirst_ref,
    dsecond_ref,
    slope_ref,
    keys,
    values,
    penalty,
    dkt,
    dvt,
):
    first, length = meta[0], meta[1]
    odd = lax.rem(first // BLOCK, 2)
    fill_keys(first_ref, keys, values, odd * BLOCK, first + (2 * odd - 1) * BLOCK, length)
    fill_keys(second_ref, keys, values, (1 - odd) * BLOCK, first - (2 * odd - 1) * BLOCK, length)
    fill_penalty(slopes_ref, penalty, [p for p in range(9) if p != BLOCK // TILE])
    dkt[...] = jnp.zeros_like(dkt)
    dvt[...] = jnp.zeros_like(dvt)
    shape = (TILE, LANES)
    lane = iota(shape, 1)

    def penalty_of(tile, head):
        low = penalty[head, :, pl.ds(0, BLOCK - tile * TILE)]
        high = penalty[head, :, pl.ds(2 * BLOCK - tile * TILE, (tile + 1) * TILE)]
        return jnp.concatenate([low, high], axis=1)

    def score(c, tile, head):
        c["span"] = pl.ds(tile * TILE, HALO)
        c["query"] = load_queries(qd_ref, bias_ref, tile)
        rows = with_spare(head, c["query"], (1.0,)).astype(BF16)
        scores = dot_nt(rows, keys[head, c["span"]]) * (FACTOR * LOG2E)
        c["scores"] = scores - penalty_of(tile, head)

    def soften(c, tile, head):
        scores = c.pop("scores")
        held = o_ref[head, pl.ds(tile * TILE, TILE)]
        top_held = held[:, spare(head) + 1 : spare(head) + 2]
        top = jnp.maximum(top_held, jnp.max(scores, axis=1, keepdims=True))
        c["powers"] = jnp.exp2(scores - top).astype(BF16)
        c["kept"] = jnp.exp2(top_held - top)

    def weigh(c, tile, head):
        held = o_ref[head, pl.ds(tile * TILE, TILE)]
        out = held * c["kept"] + dot_nn(c["powers"], values[head, c["span"]])
        c["inverse"] = 1.0 / out[:, spare(head) : spare(head) + 1]
        c["out"] = out * c["inverse"]

    def grade(c, tile, head):
        upstream = load_upstream(qd_ref, tile, first, length)
        c["upstream"] = upstream
        own = own_lanes(head, shape)
        c["delta"] = jnp.sum(jnp.where(own, upstream * c["out"], 0.0), axis=1, keepdims=True)
        up_rows = with_spare(head, upstream, thirds(-c["delta"])).astype(BF16)
        c["slope_grads"] = dot_nt(up_rows, values[head, c["span"]])

    def scale(c, tile, head):
        slope_grads = c["powers"].astype(F32) * c.pop("slope_grads")
        c["grads"] = slope_grads.astype(BF16)
        by_lane = lane_sums(slope_grads * penalty_of(tile, head)) * c["inverse"]
        c["slope"] = jnp.sum(by_lane, axis=0, keepdims=True)

    def spread(c, tile, head):
        inverse = c["inverse"]
        c["dq"] = dot_nn(c["grads"], keys[head, c["span"]]) * (inverse * FACTOR)
        part = pl.ds(head * HEAD, HEAD)
        up_cols = (c["upstream"] * inverse).T[head_half(head)].astype(BF16)
        query_cols = (c["query"] * (inverse * FACTOR)).T[head_half(head)].astype(BF16)
        dvt[part, c["span"]] += dot_nn(up_cols, c.pop("powers"))
        dkt[part, c["span"]] += dot_nn(query_cols, c.pop("grads"))

    def finish(c, tile, head):
        if head == 0:
            c_first[tile] = c
            return
        pair = (c_first[tile], c)
        rows = pl.ds(tile * TILE, TILE)
        place = first + tile * TILE + iota(shape, 0)
        context = jnp.where(lane < HEAD, pair[0]["out"], pair[1]["out"])
        ctx_ref[rows] = jnp.where(place < length, context, 0.0).astype(BF16)
        dq_ref[rows] = jnp.where(lane < HEAD, pair[0]["dq"], pair[1]["dq"])
        stats = jnp.zeros(shape, F32)
        for k in range(2):
            stats = jnp.where(lane == 2 * k, pair[k]["delta"], stats)
            stats = jnp.where(lane == 2 * k + 1, pair[k]["kept"] * pair[k]["inverse"], stats)
        stat_ref[rows] = stats

    c_first = {}
    chains = staggered([score, soften, weigh, grade, scale, spread, finish])
    for head in range(2):
        total = sum(c["slope"] for c in chains if c["head"] == head)
        slope_ref[pl.ds(head * 8, 8)] = jnp.broadcast_to(total, (8, LANES))
    for peer in range(PEERS):
        for side, out_ref in ((odd, dfirst_ref), (1 - odd, dsecond_ref)):
            cols = pl.ds(pl.multiple_of(side * BLOCK + peer * CHUNK, CHUNK), CHUNK)
            out_ref[peer, 0] = dkt[:, cols].T.astype(BF16)
            out_ref[peer, 1] = dvt[:, cols].T.astype(BF16)


def centre_backward(
    meta,
    slopes_ref,
    kv_ref,
    qd_ref,
    bias_ref,
    p_ref,
    stat_ref,
    ctx_ref,
    dq_ref,
    halo_slope_ref,
    cq_ref,
    dkv_ref,
    sums_ref,
    keys,
    values,
    penalty,
    dkt,
    dvt,
):
    first, length = meta[0], meta[1]
    fill_keys(kv_ref, keys, values, 0, first, length)
    fill_penalty(slopes_ref, penalty, range(1, 2 * BLOCK // TILE))
    dkt[...] = jnp.zeros_like(dkt)
    dvt[...] = jnp.zeros_like(dvt)
    shape = (TILE, LANES)
    lane = iota(shape, 1)

    def grade(c, tile, head):
        stats = stat_ref[pl.ds(tile * TILE, TILE)]
        delta = stats[:, 2 * head : 2 * head + 1]
        c["scale"] = stats[:, 2 * head + 1 : 2 * head + 2]
        c["upstream"] = load_upstream(qd_ref, tile, first, length)
        up_rows = with_spare(head, c["upstream"], thirds(-delta)).astype(BF16)
        c["slope_grads"] = dot_nt(up_rows, values[head])

    def scale(c, tile, head):
        c["powers"] = p_ref[head, pl.ds(tile * TILE, TILE)]
        slope_grads = c["powers"].astype(F32) * c.pop("slope_grads")
        c["grads"] = slope_grads.astype(BF16)
        far = penalty[head, :, pl.ds(BLOCK - tile * TILE, BLOCK)]
        c["slope"] = jnp.sum(lane_sums(slope_grads * far) * c["scale"], axis=0, keepdims=True)

    def spread(c, tile, head):
        ratio = c["scale"]
        c["dq"] = dot_nn(c["grads"], keys[head]) * (ratio * FACTOR)
        part = pl.ds(head * HEAD, HEAD)
        query = load_queries(qd_ref, bias_ref, tile)
        up_cols = (c["upstream"] * ratio).T[head_half(head)].astype(BF16)
        query_cols = (query * (ratio * FACTOR)).T[head_half(head)].astype(BF16)
        dvt[part] += dot_nn(up_cols, c.pop("powers"))
        dkt[part] += dot_nn(query_cols, c.pop("grads"))

    def finish(c, tile, head):
        if head == 0:
            c_first[tile] = c
            return
        dq = jnp.where(lane < HEAD, c_first[tile]["dq"], c["dq"])
        dq = dq + dq_ref[pl.ds(tile * TILE, TILE)]
        c["bias"] = jnp.sum(dq, axis=0, keepdims=True)
        for half in range(2):
            rows = slice(half * CHUNK, (half + 1) * CHUNK)
            cq_ref[2 * tile + half, 0] = ctx_ref[pl.ds(tile * TILE + half * CHUNK, CHUNK)]
            cq_ref[2 * tile + half, 1] = dq[rows].astype(BF16)

    c_first = {}
    chains = staggered([grade, scale, spread, finish])
    bias_sum = sum(c["bias"] for c in chains if c["head"] == 1)
    row = iota((1, LANES), 1)
    totals = []
    for head in range(2):
        total = sum(c["slope"] for c in chains if c["head"] == head)
        total = jnp.sum(total + halo_slope_ref[pl.ds(head * 8, 1)], axis=1, keepdims=True)
        totals.append(-total / (slopes_ref[head] * LOG2E))
    slope_sum = jnp.where(row == 0, totals[0], jnp.where(row == 1, totals[1], 0.0))
    sums = jnp.concatenate([bias_sum, slope_sum], axis=0)
    for block in range(sums_ref.shape[0]):
        sums_ref[block] = sums
    for peer in range(PEERS):
        cols = pl.ds(peer * CHUNK, CHUNK)
        dkv_ref[peer, 0] = dkt[:, cols].T
        dkv_ref[peer, 1] = dvt[:, cols].T


SMEM = pl.BlockSpec(memory_space=pltpu.SMEM)
VMEM = pl.BlockSpec(memory_space=pltpu.VMEM)
PAIR = (PEERS, 2, CHUNK, LANES)


def params():
    return pltpu.CompilerParams(vmem_limit_bytes=VMEM_LIMIT)


def small():
    return pltpu.CompilerParams(vmem_limit_bytes=12 * 1024 * 1024)


def cost(keys, products):
    pairs = 2 * BLOCK * keys
    return pl.CostEstimate(
        flops=2 * pairs * LANES * products, bytes_accessed=8 * 1024 * 1024, transcendentals=pairs
    )


def shaped(shape, kind):
    return jax.ShapeDtypeStruct(shape, kind)


def run_centre_forward(meta, slopes, kv, qd, bias):
    return pl.pallas_call(
        centre_forward,
        in_specs=[SMEM, SMEM] + [VMEM] * 3,
        out_specs=[VMEM] * 2,
        out_shape=[shaped((2, BLOCK, BLOCK), BF16), shaped((2, BLOCK, LANES), F32)],
        scratch_shapes=[
            pltpu.VMEM((2, BLOCK, LANES), BF16),
            pltpu.VMEM((2, BLOCK, LANES), BF16),
            pltpu.VMEM((2, TILE, 2 * BLOCK + TILE), F32),
        ],
        compiler_params=params(),
        cost_estimate=pl.CostEstimate(flops=1000, bytes_accessed=1000, transcendentals=0),
        name="centre_forward",
    )(meta, slopes, kv, qd, bias)


def run_halo(meta, slopes, kv_first, kv_second, qd, bias, held):
    return pl.pallas_call(
        halo_both,
        in_specs=[SMEM, SMEM] + [VMEM] * 5,
        out_specs=[VMEM] * 6,
        out_shape=[
            shaped((BLOCK, LANES), BF16),
            shaped((BLOCK, LANES), F32),
            shaped((BLOCK, LANES), F32),
            shaped(PAIR, BF16),
            shaped(PAIR, BF16),
            shaped((16, LANES), F32),
        ],
        scratch_shapes=[
            pltpu.VMEM((2, 2 * BLOCK, LANES), BF16),
            pltpu.VMEM((2, 2 * BLOCK, LANES), BF16),
            pltpu.VMEM((2, TILE, 2 * BLOCK + TILE), F32),
            pltpu.VMEM((LANES, 2 * BLOCK), F32),
            pltpu.VMEM((LANES, 2 * BLOCK), F32),
        ],
        compiler_params=params(),
        cost_estimate=cost(HALO, 6),
        name="halo_both",
    )(meta, slopes, kv_second, kv_first, qd, bias, held)


def run_centre_backward(meta, slopes, kv, qd, bias, powers, stats, context, dq, halo_slope):
    return pl.pallas_call(
        centre_backward,
        in_specs=[SMEM, SMEM] + [VMEM] * 8,
        out_specs=[VMEM] * 3,
        out_shape=[
            shaped(PAIR, BF16),
            shaped(PAIR, F32),
            shaped((lax.axis_size("blk"), 2, LANES), F32),
        ],
        scratch_shapes=[
            pltpu.VMEM((2, BLOCK, LANES), BF16),
            pltpu.VMEM((2, BLOCK, LANES), BF16),
            pltpu.VMEM((2, TILE, 2 * BLOCK + TILE), F32),
            pltpu.VMEM((LANES, BLOCK), F32),
            pltpu.VMEM((LANES, BLOCK), F32),
        ],
        compiler_params=params(),
        cost_estimate=pl.CostEstimate(flops=1000, bytes_accessed=1000, transcendentals=0),
        name="centre_backward",
    )(meta, slopes, kv, qd, bias, powers, stats, context, dq, halo_slope)


def split_pair(first_ref, second_ref, out_ref):
    for peer in range(PEERS):
        cols = pl.ds(peer * LANES, LANES)
        out_ref[peer, 0] = first_ref[0, :, cols]
        out_ref[peer, 1] = second_ref[0, :, cols]


def run_split(first, second):
    return pl.pallas_call(split_pair, out_shape=shaped(PAIR, BF16), compiler_params=small(), name="split_pair")(first, second)


def gather_grads(cq_ref, dkv_ref, first_ref, second_ref, out_ref):
    for peer in range(PEERS):
        for part in range(2):
            out_ref[peer, part] = cq_ref[peer, part]
            passed = first_ref[peer, part].astype(F32) + second_ref[peer, part].astype(F32)
            out_ref[peer, 2 + part] = (dkv_ref[peer, part] + passed).astype(BF16)


def run_gather(cq, dkv, from_first, from_second):
    return pl.pallas_call(
        gather_grads,
        out_shape=shaped((PEERS, 4, CHUNK, LANES), BF16),
        compiler_params=small(),
        name="gather_grads",
    )(cq, dkv, from_first, from_second)


def join_four(parts_ref, *out_refs):
    for peer in range(PEERS):
        cols = pl.ds(peer * LANES, LANES)
        for part in range(4):
            out_refs[part][0, :, cols] = parts_ref[peer, part]


def run_join(parts):
    whole_rows = shaped((1, CHUNK, PEERS * LANES), BF16)
    return pl.pallas_call(join_four, out_shape=[whole_rows] * 4, compiler_params=small(), name="join_four")(parts)


def across(pair):
    return lax.all_to_all(pair, "uly", split_axis=0, concat_axis=0, tiled=True)


def over_recordings(partial):
    around = [(i, i ^ 1) for i in range(4)], [(i, i ^ 2) for i in range(4)], [(i, i ^ 3) for i in range(4)]
    one, two, three = (lax.ppermute(partial, "dp", route) for route in around)
    return (partial + one) + (two + three)


def swapped(block, lowest):
    pairs = [(i, i + 1) for i in range(lowest, lax.axis_size("blk") - 1, 2)]
    return lax.ppermute(block, "blk", pairs + [(high, low) for low, high in pairs])


def local(queries, key_vectors, value_vectors, grad_context, content_bias, slopes, lengths):
    kv = across(run_split(key_vectors, value_vectors))
    kv_first = swapped(kv, 1)
    kv_second = swapped(kv, 0)
    qd = across(run_split(queries, grad_context))
    start = (lax.axis_index("blk") * BLOCK).astype(jnp.int32)
    meta = jnp.stack([start, lengths[0]])
    bias = content_bias.reshape(1, LANES)
    powers, held = run_centre_forward(meta, slopes, kv, qd, bias)
    context, dq, stats, dfirst, dsecond, halo_slope = run_halo(
        meta, slopes, kv_first, kv_second, qd, bias, held
    )
    from_first = swapped(dfirst, 1)
    from_second = swapped(dsecond, 0)
    cq, dkv, sums = run_centre_backward(
        meta, slopes, kv, qd, bias, powers, stats, context, dq, halo_slope
    )
    spread = lax.all_to_all(sums, "blk", split_axis=0, concat_axis=0, tiled=True)
    partial = jnp.sum(spread, axis=0)
    grads = run_gather(cq, dkv, from_first, from_second)
    context_out, query_out, key_out, value_out = run_join(across(grads))
    total = over_recordings(partial)
    return (
        context_out,
        query_out,
        key_out,
        value_out,
        total[0].reshape(2, HEAD),
        total[1, :2],
    )


def solution(mesh):
    rows = P("dp", ("blk", "uly"), None)
    return jax.shard_map(
        local,
        mesh=mesh,
        in_specs=(rows, rows, rows, rows, P("uly", None), P("uly"), P("dp")),
        out_specs=(rows, rows, rows, rows, P("uly", None), P("uly")),
        check_vma=False,
    )
```

```python
import jax
import jax.numpy as jnp
from jax import lax
from jax.experimental import pallas as pl
from jax.experimental.pallas import tpu as pltpu
from jax.sharding import PartitionSpec as P

BLOCK = 1024
TILE = 256
TILES = BLOCK // TILE
HALO = BLOCK + TILE
PEERS = 8
CHUNK = BLOCK // PEERS
LANES = 128
HEAD = 64
FACTOR = HEAD**-0.5
LOG2E = 1.4426950408889634
FAR = 1e30
VMEM_LIMIT = 40 * 1024 * 1024
F32 = jnp.float32
BF16 = jnp.bfloat16


def iota(shape, dim):
    return lax.broadcasted_iota(jnp.int32, shape, dim)


def dot_nt(a, b):
    return lax.dot_general(a, b, (((1,), (1,)), ((), ())), preferred_element_type=F32)


def dot_nn(a, b):
    return jnp.dot(a, b, preferred_element_type=F32)


def own_lanes(head, shape):
    lane = iota(shape, 1)
    return lane < HEAD if head == 0 else lane >= HEAD


def spare(head):
    return HEAD if head == 0 else 0


def fill_keys(kv_ref, keys, values, base, start, length):
    shape = (CHUNK, LANES)
    lane = iota(shape, 1)
    for peer in range(PEERS):
        rows = pl.ds(pl.multiple_of(base + peer * CHUNK, CHUNK), CHUNK)
        place = start + peer * CHUNK + iota(shape, 0)
        blocked = jnp.where((place >= 0) & (place < length), 0.0, -FAR)
        key = kv_ref[peer, 0].astype(F32)
        value = kv_ref[peer, 1].astype(F32)
        for head in range(2):
            own, at = own_lanes(head, shape), spare(head)
            keys[head, rows] = jnp.where(own, key, jnp.where(lane == at, blocked, 0.0)).astype(BF16)
            ones = ((lane >= at) & (lane < at + 3)).astype(F32)
            values[head, rows] = jnp.where(own, value, ones).astype(BF16)


def fill_penalty(slopes_ref, penalty, pieces):
    for piece in pieces:
        spacing = jnp.abs(iota((TILE, TILE), 0) + BLOCK - piece * TILE - iota((TILE, TILE), 1))
        for head in range(2):
            cost_here = spacing.astype(F32) * (slopes_ref[head] * LOG2E)
            if piece in (0, 2 * BLOCK // TILE):
                cost_here = jnp.where(spacing <= BLOCK, cost_here, FAR)
            penalty[head, :, pl.ds(piece * TILE, TILE)] = cost_here


def load_queries(qd_ref, bias_ref, tile):
    query = jnp.concatenate([qd_ref[2 * tile, 0], qd_ref[2 * tile + 1, 0]], axis=0).astype(F32)
    return (query + bias_ref[...]).astype(BF16).astype(F32)


def load_upstream(qd_ref, tile, first, length):
    upstream = jnp.concatenate([qd_ref[2 * tile, 1], qd_ref[2 * tile + 1, 1]], axis=0).astype(F32)
    place = first + tile * TILE + iota((TILE, LANES), 0)
    return jnp.where(place < length, upstream, 0.0)


def with_spare(head, rows, columns):
    lane = iota((TILE, LANES), 1)
    other = jnp.zeros((TILE, LANES), F32)
    for k, column in enumerate(columns):
        other = jnp.where(lane == spare(head) + k, column, other)
    return jnp.where(own_lanes(head, (TILE, LANES)), rows, other)


def thirds(column):
    high = column.astype(BF16).astype(F32)
    middle = (column - high).astype(BF16).astype(F32)
    return high, middle, column - high - middle


def staggered(stages):
    chains = [{"tile": tile, "head": head} for tile in range(TILES) for head in range(2)]
    for step in range(len(chains) + len(stages) - 1):
        for depth, stage in enumerate(stages):
            if 0 <= step - depth < len(chains):
                stage(chains[step - depth], **{k: chains[step - depth][k] for k in ("tile", "head")})
    return chains


def head_half(head):
    return slice(head * HEAD, (head + 1) * HEAD)


def lane_sums(weighted):
    total = weighted[:, :LANES]
    for piece in range(1, weighted.shape[1] // LANES):
        total = total + weighted[:, piece * LANES : (piece + 1) * LANES]
    return total


def centre_forward(meta, slopes_ref, kv_ref, qd_ref, bias_ref, p_ref, o_ref, keys, values, penalty):
    fill_keys(kv_ref, keys, values, 0, meta[0], meta[1])
    fill_penalty(slopes_ref, penalty, range(1, 2 * BLOCK // TILE))

    def score(c, tile, head):
        rows = with_spare(head, load_queries(qd_ref, bias_ref, tile), (1.0,)).astype(BF16)
        far = penalty[head, :, pl.ds(BLOCK - tile * TILE, BLOCK)]
        c["scores"] = dot_nt(rows, keys[head]) * (FACTOR * LOG2E) - far

    def soften(c, tile, head):
        scores = c.pop("scores")
        c["top"] = jnp.max(scores, axis=1, keepdims=True)
        c["powers"] = jnp.exp2(scores - c["top"]).astype(BF16)

    def weigh(c, tile, head):
        rows = pl.ds(tile * TILE, TILE)
        powers = c.pop("powers")
        p_ref[head, rows] = powers
        out = dot_nn(powers, values[head])
        o_ref[head, rows] = jnp.where(iota((TILE, LANES), 1) == spare(head) + 1, c["top"], out)

    staggered([score, soften, weigh])


def halo_both(
    meta,
    slopes_ref,
    second_ref,
    first_ref,
    qd_ref,
    bias_ref,
    o_ref,
    ctx_ref,
    dq_ref,
    stat_ref,
    dfirst_ref,
    dsecond_ref,
    slope_ref,
    keys,
    values,
    penalty,
    dkt,
    dvt,
):
    first, length = meta[0], meta[1]
    odd = lax.rem(first // BLOCK, 2)
    fill_keys(first_ref, keys, values, odd * BLOCK, first + (2 * odd - 1) * BLOCK, length)
    fill_keys(second_ref, keys, values, (1 - odd) * BLOCK, first - (2 * odd - 1) * BLOCK, length)
    fill_penalty(slopes_ref, penalty, [p for p in range(9) if p != BLOCK // TILE])
    dkt[...] = jnp.zeros_like(dkt)
    dvt[...] = jnp.zeros_like(dvt)
    shape = (TILE, LANES)
    lane = iota(shape, 1)

    def penalty_of(tile, head):
        low = penalty[head, :, pl.ds(0, BLOCK - tile * TILE)]
        high = penalty[head, :, pl.ds(2 * BLOCK - tile * TILE, (tile + 1) * TILE)]
        return jnp.concatenate([low, high], axis=1)

    def score(c, tile, head):
        c["span"] = pl.ds(tile * TILE, HALO)
        c["query"] = load_queries(qd_ref, bias_ref, tile)
        rows = with_spare(head, c["query"], (1.0,)).astype(BF16)
        scores = dot_nt(rows, keys[head, c["span"]]) * (FACTOR * LOG2E)
        c["scores"] = scores - penalty_of(tile, head)

    def soften(c, tile, head):
        scores = c.pop("scores")
        held = o_ref[head, pl.ds(tile * TILE, TILE)]
        top_held = held[:, spare(head) + 1 : spare(head) + 2]
        top = jnp.maximum(top_held, jnp.max(scores, axis=1, keepdims=True))
        c["powers"] = jnp.exp2(scores - top).astype(BF16)
        c["kept"] = jnp.exp2(top_held - top)

    def weigh(c, tile, head):
        held = o_ref[head, pl.ds(tile * TILE, TILE)]
        out = held * c["kept"] + dot_nn(c["powers"], values[head, c["span"]])
        c["inverse"] = 1.0 / out[:, spare(head) : spare(head) + 1]
        c["out"] = out * c["inverse"]

    def grade(c, tile, head):
        upstream = load_upstream(qd_ref, tile, first, length)
        c["upstream"] = upstream
        own = own_lanes(head, shape)
        c["delta"] = jnp.sum(jnp.where(own, upstream * c["out"], 0.0), axis=1, keepdims=True)
        up_rows = with_spare(head, upstream, thirds(-c["delta"])).astype(BF16)
        c["slope_grads"] = dot_nt(up_rows, values[head, c["span"]])

    def scale(c, tile, head):
        slope_grads = c["powers"].astype(F32) * c.pop("slope_grads")
        c["grads"] = slope_grads.astype(BF16)
        by_lane = lane_sums(slope_grads * penalty_of(tile, head)) * c["inverse"]
        c["slope"] = jnp.sum(by_lane, axis=0, keepdims=True)

    def spread(c, tile, head):
        inverse = c["inverse"]
        c["dq"] = dot_nn(c["grads"], keys[head, c["span"]]) * (inverse * FACTOR)
        part = pl.ds(head * HEAD, HEAD)
        up_cols = (c["upstream"] * inverse).T[head_half(head)].astype(BF16)
        query_cols = (c["query"] * (inverse * FACTOR)).T[head_half(head)].astype(BF16)
        dvt[part, c["span"]] += dot_nn(up_cols, c.pop("powers"))
        dkt[part, c["span"]] += dot_nn(query_cols, c.pop("grads"))

    def finish(c, tile, head):
        if head == 0:
            c_first[tile] = c
            return
        pair = (c_first[tile], c)
        rows = pl.ds(tile * TILE, TILE)
        place = first + tile * TILE + iota(shape, 0)
        context = jnp.where(lane < HEAD, pair[0]["out"], pair[1]["out"])
        ctx_ref[rows] = jnp.where(place < length, context, 0.0).astype(BF16)
        dq_ref[rows] = jnp.where(lane < HEAD, pair[0]["dq"], pair[1]["dq"])
        stats = jnp.zeros(shape, F32)
        for k in range(2):
            stats = jnp.where(lane == 2 * k, pair[k]["delta"], stats)
            stats = jnp.where(lane == 2 * k + 1, pair[k]["kept"] * pair[k]["inverse"], stats)
        stat_ref[rows] = stats

    c_first = {}
    chains = staggered([score, soften, weigh, grade, scale, spread, finish])
    for head in range(2):
        total = sum(c["slope"] for c in chains if c["head"] == head)
        slope_ref[pl.ds(head * 8, 8)] = jnp.broadcast_to(total, (8, LANES))
    for peer in range(PEERS):
        for side, out_ref in ((odd, dfirst_ref), (1 - odd, dsecond_ref)):
            cols = pl.ds(pl.multiple_of(side * BLOCK + peer * CHUNK, CHUNK), CHUNK)
            out_ref[peer, 0] = dkt[:, cols].T.astype(BF16)
            out_ref[peer, 1] = dvt[:, cols].T.astype(BF16)


def centre_backward(
    meta,
    slopes_ref,
    kv_ref,
    qd_ref,
    bias_ref,
    p_ref,
    stat_ref,
    ctx_ref,
    dq_ref,
    halo_slope_ref,
    cq_ref,
    dkv_ref,
    sums_ref,
    keys,
    values,
    penalty,
    dkt,
    dvt,
):
    first, length = meta[0], meta[1]
    fill_keys(kv_ref, keys, values, 0, first, length)
    fill_penalty(slopes_ref, penalty, range(1, 2 * BLOCK // TILE))
    dkt[...] = jnp.zeros_like(dkt)
    dvt[...] = jnp.zeros_like(dvt)
    shape = (TILE, LANES)
    lane = iota(shape, 1)

    def grade(c, tile, head):
        stats = stat_ref[pl.ds(tile * TILE, TILE)]
        delta = stats[:, 2 * head : 2 * head + 1]
        c["scale"] = stats[:, 2 * head + 1 : 2 * head + 2]
        c["upstream"] = load_upstream(qd_ref, tile, first, length)
        up_rows = with_spare(head, c["upstream"], thirds(-delta)).astype(BF16)
        c["slope_grads"] = dot_nt(up_rows, values[head])

    def scale(c, tile, head):
        c["powers"] = p_ref[head, pl.ds(tile * TILE, TILE)]
        slope_grads = c["powers"].astype(F32) * c.pop("slope_grads")
        c["grads"] = slope_grads.astype(BF16)
        far = penalty[head, :, pl.ds(BLOCK - tile * TILE, BLOCK)]
        c["slope"] = jnp.sum(lane_sums(slope_grads * far) * c["scale"], axis=0, keepdims=True)

    def spread(c, tile, head):
        ratio = c["scale"]
        c["dq"] = dot_nn(c["grads"], keys[head]) * (ratio * FACTOR)
        part = pl.ds(head * HEAD, HEAD)
        query = load_queries(qd_ref, bias_ref, tile)
        up_cols = (c["upstream"] * ratio).T[head_half(head)].astype(BF16)
        query_cols = (query * (ratio * FACTOR)).T[head_half(head)].astype(BF16)
        dvt[part] += dot_nn(up_cols, c.pop("powers"))
        dkt[part] += dot_nn(query_cols, c.pop("grads"))

    def finish(c, tile, head):
        if head == 0:
            c_first[tile] = c
            return
        dq = jnp.where(lane < HEAD, c_first[tile]["dq"], c["dq"])
        dq = dq + dq_ref[pl.ds(tile * TILE, TILE)]
        c["bias"] = jnp.sum(dq, axis=0, keepdims=True)
        for half in range(2):
            rows = slice(half * CHUNK, (half + 1) * CHUNK)
            cq_ref[2 * tile + half, 0] = ctx_ref[pl.ds(tile * TILE + half * CHUNK, CHUNK)]
            cq_ref[2 * tile + half, 1] = dq[rows].astype(BF16)

    c_first = {}
    chains = staggered([grade, scale, spread, finish])
    bias_sum = sum(c["bias"] for c in chains if c["head"] == 1)
    row = iota((1, LANES), 1)
    totals = []
    for head in range(2):
        total = sum(c["slope"] for c in chains if c["head"] == head)
        total = jnp.sum(total + halo_slope_ref[pl.ds(head * 8, 1)], axis=1, keepdims=True)
        totals.append(-total / (slopes_ref[head] * LOG2E))
    slope_sum = jnp.where(row == 0, totals[0], jnp.where(row == 1, totals[1], 0.0))
    sums = jnp.concatenate([bias_sum, slope_sum], axis=0)
    for block in range(sums_ref.shape[0]):
        sums_ref[block] = sums
    for peer in range(PEERS):
        cols = pl.ds(peer * CHUNK, CHUNK)
        dkv_ref[peer, 0] = dkt[:, cols].T.astype(BF16)
        dkv_ref[peer, 1] = dvt[:, cols].T.astype(BF16)


SMEM = pl.BlockSpec(memory_space=pltpu.SMEM)
VMEM = pl.BlockSpec(memory_space=pltpu.VMEM)
PAIR = (PEERS, 2, CHUNK, LANES)


def params():
    return pltpu.CompilerParams(vmem_limit_bytes=VMEM_LIMIT)


def small():
    return pltpu.CompilerParams(vmem_limit_bytes=12 * 1024 * 1024)


def cost(keys, products):
    pairs = 2 * BLOCK * keys
    return pl.CostEstimate(
        flops=2 * pairs * LANES * products, bytes_accessed=8 * 1024 * 1024, transcendentals=pairs
    )


def shaped(shape, kind):
    return jax.ShapeDtypeStruct(shape, kind)


def run_centre_forward(meta, slopes, kv, qd, bias):
    return pl.pallas_call(
        centre_forward,
        in_specs=[SMEM, SMEM] + [VMEM] * 3,
        out_specs=[VMEM] * 2,
        out_shape=[shaped((2, BLOCK, BLOCK), BF16), shaped((2, BLOCK, LANES), F32)],
        scratch_shapes=[
            pltpu.VMEM((2, BLOCK, LANES), BF16),
            pltpu.VMEM((2, BLOCK, LANES), BF16),
            pltpu.VMEM((2, TILE, 2 * BLOCK + TILE), F32),
        ],
        compiler_params=params(),
        cost_estimate=pl.CostEstimate(flops=1000, bytes_accessed=1000, transcendentals=0),
        name="centre_forward",
    )(meta, slopes, kv, qd, bias)


def run_halo(meta, slopes, kv_first, kv_second, qd, bias, held):
    return pl.pallas_call(
        halo_both,
        in_specs=[SMEM, SMEM] + [VMEM] * 5,
        out_specs=[VMEM] * 6,
        out_shape=[
            shaped((BLOCK, LANES), BF16),
            shaped((BLOCK, LANES), F32),
            shaped((BLOCK, LANES), F32),
            shaped(PAIR, BF16),
            shaped(PAIR, BF16),
            shaped((16, LANES), F32),
        ],
        scratch_shapes=[
            pltpu.VMEM((2, 2 * BLOCK, LANES), BF16),
            pltpu.VMEM((2, 2 * BLOCK, LANES), BF16),
            pltpu.VMEM((2, TILE, 2 * BLOCK + TILE), F32),
            pltpu.VMEM((LANES, 2 * BLOCK), F32),
            pltpu.VMEM((LANES, 2 * BLOCK), F32),
        ],
        compiler_params=params(),
        cost_estimate=cost(HALO, 6),
        name="halo_both",
    )(meta, slopes, kv_second, kv_first, qd, bias, held)


def run_centre_backward(meta, slopes, kv, qd, bias, powers, stats, context, dq, halo_slope):
    return pl.pallas_call(
        centre_backward,
        in_specs=[SMEM, SMEM] + [VMEM] * 8,
        out_specs=[VMEM] * 3,
        out_shape=[
            shaped(PAIR, BF16),
            shaped(PAIR, BF16),
            shaped((lax.axis_size("blk"), 2, LANES), F32),
        ],
        scratch_shapes=[
            pltpu.VMEM((2, BLOCK, LANES), BF16),
            pltpu.VMEM((2, BLOCK, LANES), BF16),
            pltpu.VMEM((2, TILE, 2 * BLOCK + TILE), F32),
            pltpu.VMEM((LANES, BLOCK), F32),
            pltpu.VMEM((LANES, BLOCK), F32),
        ],
        compiler_params=params(),
        cost_estimate=pl.CostEstimate(flops=1000, bytes_accessed=1000, transcendentals=0),
        name="centre_backward",
    )(meta, slopes, kv, qd, bias, powers, stats, context, dq, halo_slope)


def split_pair(first_ref, second_ref, out_ref):
    for peer in range(PEERS):
        cols = pl.ds(peer * LANES, LANES)
        out_ref[peer, 0] = first_ref[0, :, cols]
        out_ref[peer, 1] = second_ref[0, :, cols]


def run_split(first, second):
    return pl.pallas_call(split_pair, out_shape=shaped(PAIR, BF16), name="split_pair")(first, second)


def gather_grads(cq_ref, dkv_ref, first_ref, second_ref, out_ref):
    for peer in range(PEERS):
        for part in range(2):
            out_ref[peer, part] = cq_ref[peer, part]
            passed = first_ref[peer, part].astype(F32) + second_ref[peer, part].astype(F32)
            out_ref[peer, 2 + part] = (dkv_ref[peer, part].astype(F32) + passed).astype(BF16)


def run_gather(cq, dkv, from_first, from_second):
    return pl.pallas_call(
        gather_grads,
        out_shape=shaped((PEERS, 4, CHUNK, LANES), BF16),
        compiler_params=small(),
        name="gather_grads",
    )(cq, dkv, from_first, from_second)


def join_four(parts_ref, *out_refs):
    for peer in range(PEERS):
        cols = pl.ds(peer * LANES, LANES)
        for part in range(4):
            out_refs[part][0, :, cols] = parts_ref[peer, part]


def run_join(parts):
    whole_rows = shaped((1, CHUNK, PEERS * LANES), BF16)
    return pl.pallas_call(join_four, out_shape=[whole_rows] * 4, compiler_params=small(), name="join_four")(parts)


def across(pair):
    return lax.all_to_all(pair, "uly", split_axis=0, concat_axis=0, tiled=True)


def over_recordings(partial):
    around = [(i, i ^ 1) for i in range(4)], [(i, i ^ 2) for i in range(4)], [(i, i ^ 3) for i in range(4)]
    one, two, three = (lax.ppermute(partial, "dp", route) for route in around)
    return (partial + one) + (two + three)


def swapped(block, lowest):
    pairs = [(i, i + 1) for i in range(lowest, lax.axis_size("blk") - 1, 2)]
    return lax.ppermute(block, "blk", pairs + [(high, low) for low, high in pairs])


def local(queries, key_vectors, value_vectors, grad_context, content_bias, slopes, lengths):
    kv = across(run_split(key_vectors, value_vectors))
    kv_first = swapped(kv, 1)
    kv_second = swapped(kv, 0)
    qd = across(run_split(queries, grad_context))
    start = (lax.axis_index("blk") * BLOCK).astype(jnp.int32)
    meta = jnp.stack([start, lengths[0]])
    bias = content_bias.reshape(1, LANES)
    powers, held = run_centre_forward(meta, slopes, kv, qd, bias)
    context, dq, stats, dfirst, dsecond, halo_slope = run_halo(
        meta, slopes, kv_first, kv_second, qd, bias, held
    )
    from_first = swapped(dfirst, 1)
    from_second = swapped(dsecond, 0)
    cq, dkv, sums = run_centre_backward(
        meta, slopes, kv, qd, bias, powers, stats, context, dq, halo_slope
    )
    spread = lax.all_to_all(sums, "blk", split_axis=0, concat_axis=0, tiled=True)
    partial = jnp.sum(spread, axis=0)
    grads = run_gather(cq, dkv, from_first, from_second)
    context_out, query_out, key_out, value_out = run_join(across(grads))
    total = over_recordings(partial)
    return (
        context_out,
        query_out,
        key_out,
        value_out,
        total[0].reshape(2, HEAD),
        total[1, :2],
    )


def solution(mesh):
    rows = P("dp", ("blk", "uly"), None)
    return jax.shard_map(
        local,
        mesh=mesh,
        in_specs=(rows, rows, rows, rows, P("uly", None), P("uly"), P("dp")),
        out_specs=(rows, rows, rows, rows, P("uly", None), P("uly")),
        check_vma=False,
    )
```
